32 devices in a mesh: section: 4 (over y, x), dp: 2 (over core), mp: 4 (over z).
Axes of the slice: x: 2, y: 2, z: 4, core: 2. Of those that a mesh axis runs over, the one named last changes fastest.
Arguments:
- enc_hidden: bfloat16 [2, 128, 4096], P('dp', None, ('section', 'mp')), may hold values from -32 to 32
- enc_gain: float32 [4096], replicated, may hold values from 0.1 to 1.9
- key_weight: bfloat16 [4, 4096, 2048], P('section', None, 'mp'), may hold values from -0.09375 to 0.09375
- value_weight: bfloat16 [4, 4096, 2048], P('section', None, 'mp'), may hold values from -0.25 to 0.25
- queries: bfloat16 [2, 4, 256, 2048], P('dp', 'section', None, 'mp'), may hold values from -256 to 256
- out_grad: bfloat16 [2, 4, 256, 2048], P('dp', 'section', None, 'mp'), may hold values from -4 to 4
Outputs:
- attended: bfloat16 [2, 4, 256, 2048], P('dp', 'section', None, 'mp')
- query_grad: bfloat16 [2, 4, 256, 2048], P('dp', 'section', None, 'mp')
- hidden_grad: float32 [2, 128, 4096], P('dp', None, ('section', 'mp'))
- gain_grad: float32 [4096], P(('section', 'mp'))
The draws below stay inside these ranges and needn't reach their ends.
All inputs are finite; a program needn't handle non-finite values.
Results may differ from the reference program's by a relative error of at most 0.02.
The reference program's roundings to bfloat16 on the way (of `memory`, `shares_low`, `value_grad`, `score_grad`, `key_grad`, `head_part` and `layer_grad`) count: a program that leaves them out, or rounds other values in their place, can miss the bound.
Values may be sent and summed in bfloat16 or wider, within the bound.
No kernel may reach another device: no remote copies, remote signals or barrier semaphores. Data moves between devices by JAX's collectives and lax.ppermute only.
A program may use at most 64 MiB of HBM per device.

```python
import math
import jax
import jax.numpy as jnp
from jax import lax

D = 4096
HEADS = 32
DH = 64
LE = 128
LD = 256
SEQS = 2
LAYERS = 4
N_MP = 4


def draw_enc_hidden(key, part):
    base_key, row_key, column_key = jax.random.split(key, 3)
    row_scale = 0.3 * jnp.exp(jax.random.uniform(row_key, (SEQS, LE, 1), jnp.float32, 0.0, math.log(10.0)))
    ramp = jnp.exp(math.log(3.0) * jnp.arange(D, dtype=jnp.float32) / D).reshape(1, 1, D)
    column_scale = 0.3 * ramp * jnp.exp(jax.random.uniform(column_key, (1, 1, D), jnp.float32, 0.0, math.log(10.0)))
    base = jax.random.normal(base_key, (SEQS, LE, D), jnp.float32)
    return jnp.clip(base * row_scale * column_scale, -32.0, 32.0).astype(jnp.bfloat16)


def draw_queries(key, part):
    base_key, scale_key = jax.random.split(key)
    shape = (SEQS, LAYERS, LD, HEADS, DH)
    scale_shape = (SEQS, LAYERS, LD, HEADS, 1)
    base = jax.random.normal(base_key, shape, jnp.float32)
    scale = 2.0 * jnp.exp(jax.random.uniform(scale_key, scale_shape, jnp.float32, -0.7, 0.7))
    drawn = jnp.clip(base * scale, -256.0, 256.0)
    return drawn.reshape(SEQS, LAYERS, LD, HEADS * DH).astype(jnp.bfloat16)


def block_scale(rng, dims, pieces, smallest, top_value):
    loudness, own = 1.0, jax.random.fold_in(rng, 6)
    for position, blocks in pieces:
        steps = jnp.exp(jax.random.uniform(jax.random.fold_in(own, position), (blocks,), jnp.float32, smallest / len(pieces), top_value / len(pieces)))
        loudness = loudness * jnp.repeat(steps, dims[position] // blocks).reshape([-1 if axis == position else 1 for axis in range(len(dims))])
    return loudness


def gaussian(stream_key, shape, spread, bound, cuts=(), held_as=jnp.bfloat16):
    entries = spread * jax.random.normal(stream_key, shape, jnp.float32)
    if cuts:
        entries = entries * block_scale(stream_key, shape, cuts, -0.22, 0.18)
    return jnp.clip(entries, -bound, bound).astype(held_as)


def setup_inputs(seed: int = 0) -> dict:
    key_list = jax.random.split(jax.random.key(seed), 7)
    enc_hidden = draw_enc_hidden(jax.random.fold_in(key_list[6], 71), 0)
    enc_gain = jnp.clip(1.0 + 0.18 * jax.random.normal(key_list[1], (D,), jnp.float32), 0.1, 1.9)
    key_weight = gaussian(key_list[2], (LAYERS, D, HEADS * DH), D ** -0.5, 0.09375, ((0, 4), (2, 4)))
    value_weight = gaussian(key_list[3], (LAYERS, D, HEADS * DH), (D // 8) ** -0.5, 0.25, ((0, 4), (2, 4)))
    queries = draw_queries(jax.random.fold_in(key_list[6], 71), 0)
    out_grad = gaussian(key_list[5], (SEQS, LAYERS, LD, HEADS * DH), 0.25, 4.0, ((0, 2), (1, 4), (3, 4)))
    return dict(enc_hidden=enc_hidden, enc_gain=enc_gain, key_weight=key_weight, value_weight=value_weight, queries=queries, out_grad=out_grad)


epsilon = 1e-06

def normalize(hidden):
    widened = hidden.astype(jnp.float32)
    inverse = lax.rsqrt(lax.optimization_barrier(jnp.mean(widened * widened, axis=-1, keepdims=True)) + epsilon)
    return (widened * inverse, inverse)

def rounded(array):
    return lax.optimization_barrier(array.astype(jnp.bfloat16)).astype(jnp.float32)

def layer_pass(memory, key_matrix, value_matrix, layer_queries, layer_grads):
    batch, source_length, width = memory.shape
    flat = memory.reshape(batch * source_length, width)
    keys = jnp.dot(flat, key_matrix, preferred_element_type=jnp.float32).astype(jnp.bfloat16)
    values = jnp.dot(flat, value_matrix, preferred_element_type=jnp.float32).astype(jnp.bfloat16)
    keys_wide = keys.reshape(batch, source_length, HEADS, DH).astype(jnp.float32)
    values_wide = values.reshape(batch, source_length, HEADS, DH).astype(jnp.float32)
    asked = layer_queries.reshape(batch, -1, HEADS, DH).astype(jnp.float32)
    upstream = layer_grads.reshape(batch, -1, HEADS, DH).astype(jnp.float32)
    target_length = asked.shape[1]
    factor = DH ** (-0.5)
    scores = jnp.einsum('sqhd,skhd->shqk', asked, keys_wide) * factor
    highest = lax.optimization_barrier(jnp.max(scores, axis=-1, keepdims=True))
    raised = jnp.exp(scores - highest)
    shares = raised / lax.optimization_barrier(jnp.sum(raised, axis=-1, keepdims=True))
    shares_low = rounded(shares)
    attended = jnp.einsum('shqk,skhd->sqhd', shares_low, values_wide).astype(jnp.bfloat16)
    share_grad = jnp.einsum('sqhd,skhd->shqk', upstream, values_wide)
    value_grad = jnp.einsum('shqk,sqhd->skhd', shares_low, upstream).astype(jnp.bfloat16)
    score_grad = shares * (share_grad - lax.optimization_barrier(jnp.sum(shares * share_grad, axis=-1, keepdims=True))) * factor
    score_low = rounded(score_grad)
    query_grad = jnp.einsum('shqk,skhd->sqhd', score_low, keys_wide).astype(jnp.bfloat16)
    key_grad = jnp.einsum('shqk,sqhd->skhd', score_low, asked).astype(jnp.bfloat16)
    rows = batch * source_length
    group = HEADS * DH // N_MP
    key_parts = key_grad.reshape(rows, N_MP, group).astype(jnp.float32)
    value_parts = value_grad.reshape(rows, N_MP, group).astype(jnp.float32)
    key_split = key_matrix.reshape(width, N_MP, group).astype(jnp.float32)
    value_split = value_matrix.reshape(width, N_MP, group).astype(jnp.float32)
    head_part = jnp.einsum('rgc,dgc->grd', key_parts, key_split) + jnp.einsum('rgc,dgc->grd', value_parts, value_split)
    layer_grad = rounded(lax.optimization_barrier(jnp.sum(rounded(head_part), axis=0)))
    return (attended.reshape(batch, target_length, HEADS * DH), query_grad.reshape(batch, target_length, HEADS * DH), layer_grad.reshape(batch, source_length, width))

def reference(enc_hidden, enc_gain, key_weight, value_weight, queries, out_grad):
    normed, inverse = normalize(enc_hidden)
    memory = (normed * enc_gain).astype(jnp.bfloat16)

    def layer_step(carry, inputs):
        key_matrix, value_matrix, layer_queries, layer_grads = inputs
        attended, query_grad, layer_grad = layer_pass(memory, key_matrix, value_matrix, layer_queries, layer_grads)
        return (carry + layer_grad, (attended, query_grad))
    start_total = jnp.zeros(normed.shape, jnp.float32)
    total, (attended, query_grad) = lax.scan(layer_step, start_total, (key_weight, value_weight, jnp.swapaxes(queries, 0, 1), jnp.swapaxes(out_grad, 0, 1)))
    attended = jnp.swapaxes(attended, 0, 1)
    query_grad = jnp.swapaxes(query_grad, 0, 1)
    gain_grad = lax.optimization_barrier(jnp.sum(total * normed, axis=(0, 1))) / SEQS
    scaled = total * enc_gain
    hidden_grad = inverse * (scaled - normed * lax.optimization_barrier(jnp.mean(scaled * normed, axis=-1, keepdims=True)))
    return (attended, query_grad, hidden_grad, gain_grad)
```

```python
import jax
import jax.numpy as jnp
from jax import lax
from jax.experimental import pallas as pl
from jax.experimental.pallas import tpu as pltpu
from jax.sharding import PartitionSpec as P

DH = 64
EPSILON = 1e-06
BLOCK = 256
EXTRA = 16
EXTRA_WIDTH = 256
F32 = jnp.float32
BF16 = jnp.bfloat16
VMEM = pl.BlockSpec(memory_space=pltpu.VMEM)
SMEM = pl.BlockSpec(memory_space=pltpu.SMEM)
HBM = pl.BlockSpec(memory_space=pltpu.HBM)

NN = (((1,), (0,)), ((), ()))
NT = (((1,), (1,)), ((), ()))


def dot(a, b, dims=NN):
    return lax.dot_general(a, b, dims, preferred_element_type=F32)


def split_rows(row):
    high = row.astype(BF16)
    low = (row - high.astype(F32)).astype(BF16)
    return high, low


def in_vmem(array):
    return pltpu.with_memory_space_constraint(array, pltpu.VMEM)


def in_hbm(array):
    return pltpu.with_memory_space_constraint(array, pltpu.HBM)


def load_weights(place, wk, wv, gain, sections, slots):
    width, columns = wk.shape
    blocks = sections * slots
    block = width // blocks

    def kernel(place_ref, wk_ref, wv_ref, gain_ref, wk_out, wv_out, gain_out, sems):
        copies = []
        for j in range(sections):
            for i in range(slots):
                n = j * slots + i
                b = lax.bitwise_xor(place_ref[0], j) * slots + lax.bitwise_xor(place_ref[1], i)
                source = pl.ds(pl.multiple_of(b * block, block), block)
                copies += [
                    pltpu.make_async_copy(wk_ref.at[source, :], wk_out.at[n], sems.at[0, n]),
                    pltpu.make_async_copy(wv_ref.at[source, :], wv_out.at[n], sems.at[1, n]),
                ]
                gain_out[n] = gain_ref[b]
        for copy in copies:
            copy.start()
        for copy in copies:
            copy.wait()

    return pl.pallas_call(
        kernel,
        out_shape=(
            pltpu.VMEM((blocks, block, columns), BF16),
            pltpu.VMEM((blocks, block, columns), BF16),
            pltpu.VMEM((blocks, 1, block), F32),
        ),
        in_specs=[SMEM, HBM, HBM, VMEM],
        out_specs=(VMEM, VMEM, VMEM),
        scratch_shapes=[pltpu.SemaphoreType.DMA((2, blocks))],
        compiler_params=pltpu.CompilerParams(vmem_limit_bytes=4 << 20),
        cost_estimate=pl.CostEstimate(
            flops=0, bytes_accessed=8 * width * columns, transcendentals=0
        ),
        name="load_weights",
    )(place, in_hbm(wk), in_hbm(wv), gain)


def attend(x, gain, wk, wv, q, g):
    sections = len(x)
    slots, rows, block = x[0].shape
    length, columns = q.shape
    width = sections * slots * block
    pair = 2 * DH
    pairs = columns // pair
    factor = DH ** (-0.5)

    def kernel(*refs):
        x_refs = refs[:sections]
        (gain_ref, wk_ref, wv_ref, q_ref, g_ref, low_ref, grad_low_ref, keys_ref, values_ref,
         kg_ref, vg_ref, inverse_ref, extra_ref, memory_buf) = refs[sections:]

        squares = jnp.zeros((rows, block), F32)
        for x_ref in x_refs:
            for i in range(slots):
                wide = x_ref[i].astype(F32)
                squares += wide * wide
        inverse = lax.rsqrt(jnp.sum(squares, axis=-1, keepdims=True) / width + EPSILON)
        inverse_ref[...] = jnp.broadcast_to(inverse, inverse_ref.shape)

        keys = jnp.zeros((rows, columns), F32)
        values = jnp.zeros((rows, columns), F32)
        for j in range(sections):
            for i in range(slots):
                memory = x_refs[j][i].astype(F32) * inverse * gain_ref[j * slots + i]
                memory_buf[:, i * block:(i + 1) * block] = memory.astype(BF16)
            span = slice(j * slots, (j + 1) * slots)
            keys += dot(memory_buf[...], wk_ref[span].reshape(slots * block, columns))
            values += dot(memory_buf[...], wv_ref[span].reshape(slots * block, columns))
        keys_ref[...] = keys.astype(BF16)
        values_ref[...] = values.astype(BF16)

        first = lax.broadcasted_iota(jnp.int32, (rows, pair), 1) < DH
        zero = jnp.zeros((rows, pair), BF16)
        c_sum = jnp.zeros((rows, pair), F32)
        for p in range(pairs):
            at = slice(p * pair, (p + 1) * pair)
            k, v = keys_ref[:, at], values_ref[:, at]
            q, g = q_ref[:, at], g_ref[:, at]
            k_two = jnp.concatenate((jnp.where(first, k, zero), jnp.where(first, zero, k)), axis=0)
            v_two = jnp.concatenate((jnp.where(first, v, zero), jnp.where(first, zero, v)), axis=0)
            scores = dot(k_two, q, NT)
            share_grad = dot(v_two, g, NT)
            for h in range(2):
                half = slice(h * rows, (h + 1) * rows)
                score = scores[half]
                raised = jnp.exp((score - jnp.max(score, axis=0, keepdims=True)) * factor)
                shares = raised * (1.0 / jnp.sum(raised, axis=0, keepdims=True))
                low_ref[p, half, :] = shares.astype(BF16)
                grads = share_grad[half]
                mean = jnp.sum(shares * grads, axis=0, keepdims=True)
                grad_low_ref[p, half, :] = (shares * (grads - mean) * factor).astype(BF16)
            vg = dot(low_ref[p], g)
            kg = dot(grad_low_ref[p], q)
            vg = jnp.where(first, vg[:rows], vg[rows:]).astype(BF16)
            kg = jnp.where(first, kg[:rows], kg[rows:]).astype(BF16)
            vg_ref[:, at] = vg
            kg_ref[:, at] = kg
            c_sum += kg.astype(F32) * k.astype(F32) + vg.astype(F32) * v.astype(F32)

        row = jnp.sum(c_sum.T, axis=0, keepdims=True)
        row = jnp.concatenate((row, jnp.zeros((1, EXTRA_WIDTH - rows), F32)), axis=1)
        high, low = split_rows(row)
        blank = jnp.zeros((EXTRA - 2, EXTRA_WIDTH), BF16)
        extra_ref[...] = jnp.concatenate((high, low, blank), axis=0)

    return pl.pallas_call(
        kernel,
        out_shape=(
            pltpu.VMEM((pairs, 2 * rows, length), BF16),
            pltpu.VMEM((pairs, 2 * rows, length), BF16),
            pltpu.VMEM((rows, columns), BF16),
            pltpu.VMEM((rows, columns), BF16),
            pltpu.VMEM((rows, columns), BF16),
            pltpu.VMEM((rows, columns), BF16),
            pltpu.VMEM((rows, 128), F32),
            pltpu.VMEM((EXTRA, EXTRA_WIDTH), BF16),
        ),
        in_specs=[VMEM] * (sections + 5),
        out_specs=(VMEM,) * 8,
        scratch_shapes=[pltpu.VMEM((rows, slots * block), BF16)],
        compiler_params=pltpu.CompilerParams(vmem_limit_bytes=16 << 20),
        cost_estimate=pl.CostEstimate(
            flops=4 * rows * width * columns + 16 * length * rows * columns,
            bytes_accessed=8 * width * columns,
            transcendentals=length * rows * columns // DH,
        ),
        name="attend",
    )(*x, gain, in_vmem(wk), in_vmem(wv), q, g)


def outputs(low, grad_low, keys, values):
    pairs, both, length = low.shape
    rows, columns = keys.shape
    pair = columns // pairs

    def kernel(low_ref, grad_low_ref, keys_ref, values_ref, attended_ref, query_grad_ref):
        first = lax.broadcasted_iota(jnp.int32, (rows, pair), 1) < DH
        zero = jnp.zeros((rows, pair), BF16)
        for p in range(pairs):
            at = slice(p * pair, (p + 1) * pair)
            for part, weight, out in (
                (low_ref, values_ref, attended_ref), (grad_low_ref, keys_ref, query_grad_ref)
            ):
                w = weight[:, at]
                two = jnp.concatenate((jnp.where(first, w, zero), jnp.where(first, zero, w)), axis=0)
                out[:, at] = dot(two.T, part[p]).T.astype(BF16)

    return pl.pallas_call(
        kernel,
        out_shape=(jax.ShapeDtypeStruct((length, columns), BF16),) * 2,
        in_specs=[VMEM] * 4,
        out_specs=(VMEM, VMEM),
        compiler_params=pltpu.CompilerParams(vmem_limit_bytes=8 << 20),
        cost_estimate=pl.CostEstimate(
            flops=8 * length * rows * columns,
            bytes_accessed=4 * length * columns + 4 * pairs * both * length,
            transcendentals=0,
        ),
        name="outputs",
    )(in_vmem(low), in_vmem(grad_low), in_vmem(keys), in_vmem(values))


def project(kg, vg, extra, wk, wv, j, slots):
    rows, columns = kg.shape
    block = wk.shape[1]

    def kernel(kg_ref, vg_ref, extra_ref, wk_ref, wv_ref, out_ref):
        kg, vg = kg_ref[...], vg_ref[...]
        for i in range(slots):
            n = j * slots + i
            part = dot(kg, wk_ref[n], NT) + dot(vg, wv_ref[n], NT)
            out_ref[i * rows:(i + 1) * rows, :] = part.astype(BF16)
        out_ref[slots * rows:, :] = extra_ref[...]

    return pl.pallas_call(
        kernel,
        out_shape=jax.ShapeDtypeStruct((slots * rows + EXTRA, block), BF16),
        in_specs=[VMEM] * 5,
        out_specs=VMEM,
        compiler_params=pltpu.CompilerParams(vmem_limit_bytes=4 << 20),
        cost_estimate=pl.CostEstimate(
            flops=4 * rows * columns * slots * block,
            bytes_accessed=4 * slots * block * columns,
            transcendentals=0,
        ),
        name="project",
    )(in_vmem(kg), in_vmem(vg), in_vmem(extra), in_vmem(wk), in_vmem(wv))


def sum_sections(chunks, slots, rows, c_rows):
    count = len(chunks)
    block = chunks[0].shape[1]

    def kernel(*refs):
        parts, outs = refs[:count], refs[count:]

        def total(start, size):
            acc = parts[0][start:start + size, :].astype(F32)
            for part in parts[1:]:
                acc += part[start:start + size, :].astype(F32)
            return acc

        extra = total(slots * rows, EXTRA)
        high, low = split_rows(extra[:c_rows] + extra[c_rows:2 * c_rows])
        blank = jnp.zeros((EXTRA - 2 * c_rows, block), BF16)
        tail = jnp.concatenate((high, low, blank), axis=0)
        for i in range(slots):
            outs[i][:rows, :] = total(i * rows, rows).astype(BF16)
            outs[i][rows:, :] = tail

    return pl.pallas_call(
        kernel,
        out_shape=(jax.ShapeDtypeStruct((rows + EXTRA, block), BF16),) * slots,
        in_specs=[VMEM] * count,
        out_specs=(VMEM,) * slots,
        compiler_params=pltpu.CompilerParams(vmem_limit_bytes=8 << 20),
        name="sum_sections",
    )(*chunks)


def finish(parts, hidden, gain, inverse, width, c_rows):
    count = len(parts)
    rows, block = hidden.shape

    def kernel(hidden_ref, gain_ref, inverse_ref, *refs):
        parts, (grad_ref, gain_grad_ref) = refs[:count], refs[count:]
        total = parts[0][...].astype(F32)
        for part in parts[1:]:
            total += part[...].astype(F32)
        extra = total[rows:]
        c = extra[:c_rows] + extra[c_rows:2 * c_rows]
        c = jnp.concatenate([c[n:n + 1] for n in range(c_rows)], axis=1)[:, :rows]
        mean = (jnp.broadcast_to(c, (rows, rows)) / width).T[:, 0:1]
        total = total[:rows]
        inverse = inverse_ref[:, 0:1]
        normed = hidden_ref[...].astype(F32) * inverse
        gain_grad_ref[...] = jnp.sum(total * normed, axis=0, keepdims=True)
        grad_ref[...] = inverse * (total * gain_ref[0] - normed * mean)

    return pl.pallas_call(
        kernel,
        out_shape=(
            jax.ShapeDtypeStruct((rows, block), F32),
            jax.ShapeDtypeStruct((1, block), F32),
        ),
        in_specs=[VMEM] * (count + 3),
        out_specs=(VMEM, VMEM),
        compiler_params=pltpu.CompilerParams(vmem_limit_bytes=8 << 20),
        name="finish",
    )(hidden, gain, in_vmem(inverse), *parts)


def partners(axis, array_of, size):
    order = sorted(range(1, size), key=lambda j: -bin(j).count("1"))
    got = {}
    for j in order:
        got[j] = lax.ppermute(array_of(j), axis, [(d, d ^ j) for d in range(size)])
    return [got[j] for j in range(1, size)]


def swapped(array, axis, mine):
    return jnp.stack(
        [
            lax.dynamic_index_in_dim(array, jnp.bitwise_xor(mine, i), axis, False)
            for i in range(array.shape[axis])
        ],
        axis,
    )


def per_device(enc_hidden, enc_gain, key_weight, value_weight, queries, out_grad):
    own = enc_hidden[0]
    rows, own_columns = own.shape
    wk, wv = key_weight[0], value_weight[0]
    width, columns = wk.shape
    sections = lax.axis_size("section")
    groups = lax.axis_size("mp")
    replicas = lax.axis_size("dp")
    section = lax.axis_index("section")
    mp = lax.axis_index("mp")
    direct = own_columns == BLOCK
    c_rows = max(rows // own_columns, 1)

    stack = jnp.stack([own] + partners("mp", lambda j: own, groups))
    gain = enc_gain.reshape(width // BLOCK, 1, BLOCK)
    if direct:
        slots = groups
        x = [stack] + partners("section", lambda j: stack, sections)
        place = jnp.stack((section, mp))
    else:
        slots = 4
        x = lax.all_gather(stack, "section", axis=0)
        x = swapped(x, 1, mp).transpose(2, 0, 1, 3).reshape(rows, -1, slots, BLOCK)
        x = list(x.transpose(1, 2, 0, 3))
        place = jnp.zeros(2, jnp.int32)
    wk, wv, gain = load_weights(place, wk, wv, gain, len(x), slots)
    low, grad_low, keys, values, kg, vg, inverse, extra = attend(
        x, gain, wk, wv, queries[0, 0], out_grad[0, 0]
    )

    if direct:
        def chunk(j):
            return project(kg, vg, extra, wk, wv, j, slots)
    else:
        whole = [project(kg, vg, extra, wk, wv, n, slots)[:-EXTRA] for n in range(len(x))]
        whole = jnp.stack(whole).reshape(-1, rows, BLOCK).transpose(1, 0, 2)
        whole = whole.reshape(rows, sections, groups, own_columns).transpose(1, 2, 0, 3)
        whole = swapped(whole, 1, mp).reshape(sections, groups * rows, own_columns)
        tail = extra[:2, : c_rows * own_columns].reshape(2 * c_rows, own_columns)
        tail = jnp.concatenate((tail, jnp.zeros((EXTRA - 2 * c_rows, own_columns), BF16)))
        gain = lax.dynamic_slice_in_dim(
            enc_gain, (section * groups + mp) * own_columns, own_columns, 0
        ).reshape(1, 1, own_columns)

        def chunk(j):
            body = lax.dynamic_index_in_dim(whole, jnp.bitwise_xor(section, j), 0, False)
            return jnp.concatenate((body, tail))

    got = partners("section", chunk, sections)
    summed = sum_sections([chunk(0)] + got, groups, rows, c_rows)
    attended, query_grad = outputs(low, grad_low, keys, values)
    got = partners("mp", lambda j: summed[j], groups)
    hidden_grad, gain_part = finish([summed[0]] + got, own, gain, inverse, width, c_rows)
    if replicas == 2:
        gain_total = gain_part + lax.ppermute(gain_part, "dp", [(0, 1), (1, 0)])
    else:
        gain_total = lax.psum(gain_part, "dp")
    return (
        attended[None, None],
        query_grad[None, None],
        hidden_grad[None],
        gain_total[0] / replicas,
    )


def solution(mesh):
    in_specs = (
        P("dp", None, ("section", "mp")),
        P(),
        P("section", None, "mp"),
        P("section", None, "mp"),
        P("dp", "section", None, "mp"),
        P("dp", "section", None, "mp"),
    )
    out_specs = (
        P("dp", "section", None, "mp"),
        P("dp", "section", None, "mp"),
        P("dp", None, ("section", "mp")),
        P(("section", "mp")),
    )
    return jax.shard_map(
        per_device, mesh=mesh, in_specs=in_specs, out_specs=out_specs, check_vma=False
    )
```

```python
import jax
import jax.numpy as jnp
from jax import lax
from jax.experimental import pallas as pl
from jax.experimental.pallas import tpu as pltpu
from jax.sharding import PartitionSpec as P

DH = 64
EPSILON = 1e-06
BLOCK = 256
EXTRA = 16
EXTRA_WIDTH = 256
F32 = jnp.float32
BF16 = jnp.bfloat16
VMEM = pl.BlockSpec(memory_space=pltpu.VMEM)
SMEM = pl.BlockSpec(memory_space=pltpu.SMEM)
HBM = pl.BlockSpec(memory_space=pltpu.HBM)

NN = (((1,), (0,)), ((), ()))
NT = (((1,), (1,)), ((), ()))


def dot(a, b, dims=NN):
    return lax.dot_general(a, b, dims, preferred_element_type=F32)


def split_rows(row):
    high = row.astype(BF16)
    low = (row - high.astype(F32)).astype(BF16)
    return high, low


def in_vmem(array):
    return pltpu.with_memory_space_constraint(array, pltpu.VMEM)


def cost(flops, size):
    return pl.CostEstimate(flops=flops, bytes_accessed=size, transcendentals=0)


def in_hbm(array):
    return pltpu.with_memory_space_constraint(array, pltpu.HBM)


def fetch(own, gain):
    def kernel(own_ref, gain_ref, own_out, gain_out, sems):
        copies = (
            pltpu.make_async_copy(own_ref, own_out.at[0], sems.at[0]),
            pltpu.make_async_copy(gain_ref, gain_out, sems.at[1]),
        )
        for copy in copies:
            copy.start()
        for copy in copies:
            copy.wait()

    return pl.pallas_call(
        kernel,
        out_shape=(pltpu.VMEM((1, *own.shape), BF16), pltpu.VMEM(gain.shape, F32)),
        in_specs=[HBM, HBM],
        out_specs=(VMEM, VMEM),
        scratch_shapes=[pltpu.SemaphoreType.DMA((2,))],
        compiler_params=pltpu.CompilerParams(vmem_limit_bytes=1 << 20),
        cost_estimate=cost(0, 1 << 20),
        name="fetch",
    )(in_hbm(own), in_hbm(gain))


def load_weights(place, wk, wv, gain, sections, slots):
    width, columns = wk.shape
    block = gain.shape[2]

    def kernel(place_ref, wk_ref, wv_ref, gain_ref, *refs):
        outs, sems = refs[:-1], refs[-1]
        copies = []
        for j in range(sections):
            gain_out, wk_out, wv_out = outs[j::sections]
            for i in range(slots):
                b = lax.bitwise_xor(place_ref[0], j) * slots + lax.bitwise_xor(place_ref[1], i)
                source = pl.ds(pl.multiple_of(b * block, block), block)
                n = j * slots + i
                copies += [
                    pltpu.make_async_copy(wk_ref.at[source, :], wk_out.at[i], sems.at[0, n]),
                    pltpu.make_async_copy(wv_ref.at[source, :], wv_out.at[i], sems.at[1, n]),
                ]
                gain_out[i] = gain_ref[b]
        for copy in copies:
            copy.start()
        for copy in copies:
            copy.wait()

    outs = pl.pallas_call(
        kernel,
        out_shape=(pltpu.VMEM((slots, 1, block), F32),) * sections
        + (pltpu.VMEM((slots, block, columns), BF16),) * (2 * sections),
        in_specs=[SMEM, HBM, HBM, VMEM],
        out_specs=(VMEM,) * (3 * sections),
        scratch_shapes=[pltpu.SemaphoreType.DMA((2, sections * slots))],
        compiler_params=pltpu.CompilerParams(vmem_limit_bytes=1 << 20),
        cost_estimate=cost(0, 8 * width * columns),
        name="load_weights",
    )(place, in_hbm(wk), in_hbm(wv), in_vmem(gain))
    return [outs[n * sections:(n + 1) * sections] for n in range(3)]


def attend(x, gain, wk, wv, q, g):
    sections = len(x)
    flat = [array for arrays in x for array in arrays]
    _, rows, block = flat[0].shape
    slots = sum(array.shape[0] for array in x[0])
    length, columns = q.shape
    width = sections * slots * block
    pair = 2 * DH
    pairs = columns // pair
    factor = DH ** (-0.5)

    def kernel(*refs):
        x_refs, refs = refs[:len(flat)], refs[len(flat):]
        gain_refs, wk_refs, wv_refs = (refs[n * sections:(n + 1) * sections] for n in range(3))
        (q_ref, g_ref, low_ref, grad_low_ref, keys_ref, values_ref, kg_ref, vg_ref, inverse_ref,
         extra_ref, memory_buf) = refs[3 * sections:]
        places = [(ref, i) for ref in x_refs for i in range(ref.shape[0])]

        def wide(j, i):
            ref, n = places[j * slots + i]
            return ref[n].astype(F32)

        squares = jnp.zeros((rows, block), F32)
        for j in range(sections):
            for i in range(slots):
                squares += wide(j, i) * wide(j, i)
        inverse = lax.rsqrt(jnp.sum(squares, axis=-1, keepdims=True) / width + EPSILON)
        inverse_ref[...] = jnp.broadcast_to(inverse, inverse_ref.shape)

        keys = jnp.zeros((rows, columns), F32)
        values = jnp.zeros((rows, columns), F32)
        for j in range(sections):
            for i in range(slots):
                memory = wide(j, i) * inverse * gain_refs[j][i]
                memory_buf[:, i * block:(i + 1) * block] = memory.astype(BF16)
            keys += dot(memory_buf[...], wk_refs[j][...].reshape(slots * block, columns))
            values += dot(memory_buf[...], wv_refs[j][...].reshape(slots * block, columns))
        keys_ref[...] = keys.astype(BF16)
        values_ref[...] = values.astype(BF16)

        first = lax.broadcasted_iota(jnp.int32, (rows, pair), 1) < DH
        zero = jnp.zeros((rows, pair), BF16)
        c_sum = jnp.zeros((rows, pair), F32)
        for p in range(pairs):
            at = slice(p * pair, (p + 1) * pair)
            k, v = keys_ref[:, at], values_ref[:, at]
            q, g = q_ref[:, at], g_ref[:, at]
            k_two = jnp.concatenate((jnp.where(first, k, zero), jnp.where(first, zero, k)), axis=0)
            v_two = jnp.concatenate((jnp.where(first, v, zero), jnp.where(first, zero, v)), axis=0)
            scores = dot(k_two, q, NT)
            share_grad = dot(v_two, g, NT)
            for h in range(2):
                head = slice(h * rows, (h + 1) * rows)
                score = scores[head]
                raised = jnp.exp((score - jnp.max(score, axis=0, keepdims=True)) * factor)
                shares = raised * (1.0 / jnp.sum(raised, axis=0, keepdims=True))
                low_ref[p, head, :] = shares.astype(BF16)
                grads = share_grad[head]
                mean = jnp.sum(shares * grads, axis=0, keepdims=True)
                grad_low_ref[p, head, :] = (shares * (grads - mean) * factor).astype(BF16)
            vg = dot(low_ref[p], g)
            kg = dot(grad_low_ref[p], q)
            vg = jnp.where(first, vg[:rows], vg[rows:]).astype(BF16)
            kg = jnp.where(first, kg[:rows], kg[rows:]).astype(BF16)
            vg_ref[:, at] = vg
            kg_ref[:, at] = kg
            c_sum += kg.astype(F32) * k.astype(F32) + vg.astype(F32) * v.astype(F32)

        row = jnp.sum(c_sum.T, axis=0, keepdims=True)
        row = jnp.concatenate((row, jnp.zeros((1, EXTRA_WIDTH - rows), F32)), axis=1)
        high, low = split_rows(row)
        blank = jnp.zeros((EXTRA - 2, EXTRA_WIDTH), BF16)
        extra_ref[...] = jnp.concatenate((high, low, blank), axis=0)

    return pl.pallas_call(
        kernel,
        out_shape=(
            pltpu.VMEM((pairs, 2 * rows, length), BF16),
            pltpu.VMEM((pairs, 2 * rows, length), BF16),
            pltpu.VMEM((rows, columns), BF16),
            pltpu.VMEM((rows, columns), BF16),
            pltpu.VMEM((rows, columns), BF16),
            pltpu.VMEM((rows, columns), BF16),
            pltpu.VMEM((rows, 128), F32),
            pltpu.VMEM((EXTRA, EXTRA_WIDTH), BF16),
        ),
        in_specs=[VMEM] * (len(flat) + 3 * sections + 2),
        out_specs=(VMEM,) * 8,
        scratch_shapes=[pltpu.VMEM((rows, slots * block), BF16)],
        compiler_params=pltpu.CompilerParams(vmem_limit_bytes=16 << 20),
        cost_estimate=pl.CostEstimate(
            flops=4 * rows * width * columns + 16 * length * rows * columns,
            bytes_accessed=8 * width * columns,
            transcendentals=length * rows * columns // DH,
        ),
        name="attend",
    )(*flat, *map(in_vmem, gain), *map(in_vmem, wk), *map(in_vmem, wv), q, g)


def mix(shares, weights):
    pairs, both, length = shares.shape
    rows, columns = weights.shape
    pair = columns // pairs

    def kernel(shares_ref, weights_ref, out_ref):
        first = lax.broadcasted_iota(jnp.int32, (rows, pair), 1) < DH
        zero = jnp.zeros((rows, pair), BF16)
        for p in range(pairs):
            at = slice(p * pair, (p + 1) * pair)
            w = weights_ref[:, at]
            two = jnp.concatenate((jnp.where(first, w, zero), jnp.where(first, zero, w)), axis=0)
            out_ref[:, at] = dot(two.T, shares_ref[p]).T.astype(BF16)

    return pl.pallas_call(
        kernel,
        out_shape=jax.ShapeDtypeStruct((length, columns), BF16),
        in_specs=[VMEM] * 2,
        out_specs=VMEM,
        compiler_params=pltpu.CompilerParams(vmem_limit_bytes=4 << 20),
        cost_estimate=cost(1, 1),
        name="mix",
    )(in_vmem(shares), in_vmem(weights))


def project(kg, vg, wk, wv, start, count, extra=None):
    rows, columns = kg.shape
    block = wk.shape[1]
    tail = [] if extra is None else [in_vmem(extra)]
    more = 0 if extra is None else extra.shape[0]

    def kernel(kg_ref, vg_ref, wk_ref, wv_ref, *refs):
        kg, vg, out_ref = kg_ref[...], vg_ref[...], refs[-1]
        for i in range(count):
            n = start + i
            part = dot(kg, wk_ref[n], NT) + dot(vg, wv_ref[n], NT)
            out_ref[i * rows:(i + 1) * rows, :] = part.astype(BF16)
        if tail:
            out_ref[count * rows:, :] = refs[0][...]

    return pl.pallas_call(
        kernel,
        out_shape=pltpu.VMEM((count * rows + more, block), BF16),
        in_specs=[VMEM] * (4 + len(tail)),
        out_specs=VMEM,
        compiler_params=pltpu.CompilerParams(vmem_limit_bytes=4 << 20),
        cost_estimate=cost(1, 1),
        name="project",
    )(in_vmem(kg), in_vmem(vg), in_vmem(wk), in_vmem(wv), *tail)


def join(first, second):
    count = first.shape[0]

    def kernel(first_ref, second_ref, out_ref):
        out_ref[:count] = first_ref[...]
        out_ref[count:] = second_ref[...]

    return pl.pallas_call(
        kernel,
        out_shape=pltpu.VMEM((count + second.shape[0], *first.shape[1:]), BF16),
        in_specs=[VMEM, VMEM],
        out_specs=VMEM,
        compiler_params=pltpu.CompilerParams(vmem_limit_bytes=2 << 20),
        name="join",
    )(in_vmem(first), second)


def total_of(refs, start, size):
    total = refs[0][start:start + size, :].astype(F32)
    for ref in refs[1:]:
        total += ref[start:start + size, :].astype(F32)
    return total


def sum_c(extra, c_rows):
    return extra[:c_rows] + extra[c_rows:2 * c_rows]


def c_tail(c):
    high, low = split_rows(c)
    blank = jnp.zeros((EXTRA - 2 * c.shape[0], c.shape[1]), BF16)
    return jnp.concatenate((high, low, blank), axis=0)


def sum_far(chunks, rows, c_rows):
    size, block = chunks[0].shape

    def kernel(*refs):
        parts, out = refs[:-1], refs[-1]
        for start in range(0, size - EXTRA, rows):
            out[start:start + rows, :] = total_of(parts, start, rows).astype(BF16)
        out[size - EXTRA:, :] = c_tail(sum_c(total_of(parts, size - EXTRA, EXTRA), c_rows))

    return pl.pallas_call(
        kernel,
        out_shape=pltpu.VMEM((size, block), BF16),
        in_specs=[VMEM] * len(chunks),
        out_specs=VMEM,
        compiler_params=pltpu.CompilerParams(vmem_limit_bytes=4 << 20),
        name="sum_far",
    )(*chunks)


def sum_near(chunks, mine, theirs, rows, c_rows):
    block = mine.shape[1]
    size = mine.shape[0] - EXTRA

    def kernel(mine_ref, theirs_ref, *refs):
        parts, (own_ref, out) = refs[:-2], refs[-2:]
        extra = mine_ref[size:, :].astype(F32) + theirs_ref[size:, :].astype(F32)
        out[size - rows:, :] = c_tail(sum_c(extra, c_rows))
        parts = (theirs_ref, *parts)
        own_ref[...] = total_of(parts, 0, rows)
        for start in range(rows, size, rows):
            out[start - rows:start, :] = total_of(parts, start, rows).astype(BF16)

    return pl.pallas_call(
        kernel,
        out_shape=(
            pltpu.VMEM((rows, block), F32), pltpu.VMEM((size - rows + EXTRA, block), BF16)
        ),
        in_specs=[VMEM] * (2 + len(chunks)),
        out_specs=(VMEM, VMEM),
        compiler_params=pltpu.CompilerParams(vmem_limit_bytes=4 << 20),
        name="sum_near",
    )(in_vmem(mine), theirs, *chunks)


def gain_part(own_total, part, hidden, inverse):
    rows, block = own_total.shape

    def kernel(hidden_ref, inverse_ref, own_ref, part_ref, out_ref):
        total = own_ref[...] + part_ref[:rows, :].astype(F32)
        normed = hidden_ref[0].astype(F32) * inverse_ref[:, 0:1]
        out_ref[...] = jnp.sum(total * normed, axis=0, keepdims=True)

    return pl.pallas_call(
        kernel,
        out_shape=pltpu.VMEM((1, block), F32),
        in_specs=[VMEM] * 4,
        out_specs=VMEM,
        compiler_params=pltpu.CompilerParams(vmem_limit_bytes=4 << 20),
        name="gain_part",
    )(in_vmem(hidden), in_vmem(inverse), in_vmem(own_total), part)


def finish(own_total, mine, part, hidden, gain, inverse, width, c_rows):
    rows, block = own_total.shape

    def kernel(hidden_ref, gain_ref, inverse_ref, own_ref, mine_ref, part_ref, out_ref):
        extra = mine_ref[...].astype(F32) + part_ref[rows:, :].astype(F32)
        c = sum_c(extra, c_rows)
        c = jnp.concatenate([c[n:n + 1] for n in range(c_rows)], axis=1)[:, :rows]
        mean = (jnp.broadcast_to(c, (rows, rows)) / width).T[:, 0:1]
        total = own_ref[...] + part_ref[:rows, :].astype(F32)
        inverse = inverse_ref[:, 0:1]
        normed = hidden_ref[0].astype(F32) * inverse
        out_ref[...] = inverse * (total * gain_ref[0] - normed * mean)

    return pl.pallas_call(
        kernel,
        out_shape=jax.ShapeDtypeStruct((rows, block), F32),
        in_specs=[VMEM] * 6,
        out_specs=VMEM,
        compiler_params=pltpu.CompilerParams(vmem_limit_bytes=4 << 20),
        cost_estimate=cost(0, 64 << 10),
        name="finish",
    )(in_vmem(hidden), gain, in_vmem(inverse), in_vmem(own_total), in_vmem(mine), part)


def add_gain(mine, theirs, replicas):
    def kernel(mine_ref, theirs_ref, out_ref):
        out_ref[...] = (mine_ref[...] + theirs_ref[...]) / replicas

    return pl.pallas_call(
        kernel,
        out_shape=jax.ShapeDtypeStruct(mine.shape, F32),
        in_specs=[VMEM, VMEM],
        out_specs=VMEM,
        compiler_params=pltpu.CompilerParams(vmem_limit_bytes=1 << 20),
        name="add_gain",
    )(in_vmem(mine), theirs)


def to_partner(array, axis, j):
    return lax.ppermute(array, axis, [(d, d ^ j) for d in range(lax.axis_size(axis))])


def swapped(array, axis, mine):
    return jnp.stack(
        [
            lax.dynamic_index_in_dim(array, jnp.bitwise_xor(mine, i), axis, False)
            for i in range(array.shape[axis])
        ],
        axis,
    )


def per_device(enc_hidden, enc_gain, key_weight, value_weight, queries, out_grad):
    own = enc_hidden[0]
    rows, own_columns = own.shape
    wk, wv = key_weight[0], value_weight[0]
    width, columns = wk.shape
    sections = lax.axis_size("section")
    groups = lax.axis_size("mp")
    replicas = lax.axis_size("dp")
    section = lax.axis_index("section")
    mp = lax.axis_index("mp")
    direct = own_columns == BLOCK
    c_rows = max(rows // own_columns, 1)

    half = groups // 2
    far_first = sorted(range(1, sections), key=lambda j: -bin(j).count("1"))
    place = jnp.stack((section, mp)) if direct else jnp.zeros(2, jnp.int32)
    slots = groups if direct else 4

    hidden, gain = fetch(own, enc_gain.reshape(width // BLOCK, 1, BLOCK))
    near, step = hidden, 1
    while step < half:
        near = join(near, to_partner(own[None] if step == 1 else near, "mp", step))
        step *= 2
    far = to_partner(near, "mp", half)
    if direct:
        x = [(near, far)]
        for j in range(1, sections):
            x.append((to_partner(near, "section", j), to_partner(far, "section", j)))
    else:
        x = lax.all_gather(jnp.concatenate((near, far)), "section", axis=0)
        x = swapped(x, 1, mp).transpose(2, 0, 1, 3).reshape(rows, -1, slots, BLOCK)
        x = [(part,) for part in x.transpose(1, 2, 0, 3)]
    gain, wk, wv = load_weights(place, wk, wv, gain, len(x), slots)
    low, grad_low, keys, values, kg, vg, inverse, extra = attend(
        x, gain, wk, wv, queries[0, 0], out_grad[0, 0]
    )

    if direct:
        own_gain = gain[0]
        pad = jnp.zeros((32, BLOCK), BF16)
        far = [
            project(kg, vg, wk[j], wv[j], half, slots - half, extra) for j in range(sections)
        ]
        far[1:], low = lax.optimization_barrier((far[1:], low))
    attended = mix(low, values)
    if direct:
        kg, attended = lax.optimization_barrier((kg, attended))
        near = [project(kg, vg, wk[j], wv[j], 0, half, pad) for j in range(sections)]
    else:
        whole = [
            project(kg, vg, wk[n // slots], wv[n // slots], n % slots, 1)
            for n in range(width // BLOCK)
        ]
        whole = jnp.stack(whole).transpose(1, 0, 2)
        whole = whole.reshape(rows, sections, groups, own_columns).transpose(1, 2, 0, 3)
        whole = swapped(swapped(whole, 1, mp), 0, section)
        tail = extra[:2, : c_rows * own_columns].reshape(2 * c_rows, own_columns)
        tail = jnp.concatenate((tail, jnp.zeros((EXTRA - 2 * c_rows, own_columns), BF16)))
        near = list(whole[:, :half].reshape(sections, half * rows, own_columns))
        far = whole[:, half:].reshape(sections, (groups - half) * rows, own_columns)
        far = [jnp.concatenate((part, tail)) for part in far]
        own_gain = lax.dynamic_slice_in_dim(
            enc_gain, (section * groups + mp) * own_columns, own_columns, 0
        ).reshape(1, 1, own_columns)

    far = far[:1] + [to_partner(far[j], "section", j) for j in far_first]
    near = near[:1] + [to_partner(near[j], "section", j) for j in far_first]
    mine = sum_far(far, rows, c_rows)
    theirs = to_partner(mine, "mp", half)
    mine, grad_low = lax.optimization_barrier((mine, grad_low))
    query_grad = mix(grad_low, keys)
    mine, query_grad = lax.optimization_barrier((mine, query_grad))
    own_total, part = sum_near(near, mine, theirs, rows, c_rows)
    mine = part[-EXTRA:]
    part = to_partner(part, "mp", 1)
    gain_own = gain_part(own_total, part, hidden, inverse)
    if replicas == 2:
        gain_other = lax.ppermute(gain_own, "dp", [(0, 1), (1, 0)])
    else:
        gain_other = lax.psum(gain_own, "dp")
        gain_own = jnp.zeros_like(gain_own)
    hidden_grad = finish(own_total, mine, part, hidden, own_gain, inverse, width, c_rows)
    gain_total = add_gain(gain_own, gain_other, replicas)
    return (
        attended[None, None],
        query_grad[None, None],
        hidden_grad[None],
        gain_total[0],
    )


def solution(mesh):
    in_specs = (
        P("dp", None, ("section", "mp")),
        P(),
        P("section", None, "mp"),
        P("section", None, "mp"),
        P("dp", "section", None, "mp"),
        P("dp", "section", None, "mp"),
    )
    out_specs = (
        P("dp", "section", None, "mp"),
        P("dp", "section", None, "mp"),
        P("dp", None, ("section", "mp")),
        P(("section", "mp")),
    )
    return jax.shard_map(
        per_device, mesh=mesh, in_specs=in_specs, out_specs=out_specs, check_vma=False
    )
```

```python
import math

import jax
import jax.numpy as jnp
from jax import lax
from jax.experimental import pallas as pl
from jax.experimental.pallas import tpu as pltpu
from jax.sharding import PartitionSpec as P

DH = 64
EPSILON = 1e-06
BLOCK = 256
EXTRA = 16
EXTRA_WIDTH = 256
TURN_GATHER = True
TURN_SCATTER = True
REORDER = True
F32 = jnp.float32
BF16 = jnp.bfloat16
VMEM = pl.BlockSpec(memory_space=pltpu.VMEM)
SMEM = pl.BlockSpec(memory_space=pltpu.SMEM)
HBM = pl.BlockSpec(memory_space=pltpu.HBM)

NN = (((1,), (0,)), ((), ()))
NT = (((1,), (1,)), ((), ()))


def dot(a, b, dims=NN):
    return lax.dot_general(a, b, dims, preferred_element_type=F32)


def split_rows(row):
    high = row.astype(BF16)
    low = (row - high.astype(F32)).astype(BF16)
    return high, low


def in_vmem(array):
    return pltpu.with_memory_space_constraint(array, pltpu.VMEM)


def cost(flops, size):
    return pl.CostEstimate(flops=flops, bytes_accessed=size, transcendentals=0)


def in_hbm(array):
    return pltpu.with_memory_space_constraint(array, pltpu.HBM)


def fetch(*arrays):
    count = len(arrays)

    def kernel(*refs):
        sems = refs[-1]
        copies = [
            pltpu.make_async_copy(refs[n], refs[count + n], sems.at[n]) for n in range(count)
        ]
        for copy in copies:
            copy.start()
        for copy in copies:
            copy.wait()

    return pl.pallas_call(
        kernel,
        out_shape=tuple(pltpu.VMEM(array.shape, array.dtype) for array in arrays),
        in_specs=[HBM] * count,
        out_specs=(VMEM,) * count,
        scratch_shapes=[pltpu.SemaphoreType.DMA((count,))],
        compiler_params=pltpu.CompilerParams(vmem_limit_bytes=1 << 20),
        cost_estimate=cost(0, 2 * sum(a.size * a.dtype.itemsize for a in arrays)),
        name="fetch",
    )(*map(in_hbm, arrays))


def far_first(j):
    return j ^ (j & 1) * 2


def first_row(direct, j, i, slots, block, turned, reordered):
    if direct:
        section, mp, core = (lax.axis_index(name) for name in ("section", "mp", "dp"))
        odd = lax.rem(core, 2) if turned else 0
        label = far_first if reordered else lambda n: n
        section = lax.bitwise_xor(section, j + odd * (i - j))
        mp = lax.bitwise_xor(mp, label(i) + odd * (label(j) - label(i)))
    else:
        section, mp = j, i
    return pl.multiple_of((section * slots + mp) * block, block)


def attend(x, gain, wk, wv, q, g, direct):
    sections = len(x)
    flat = [array for arrays in x for array in arrays]
    _, rows, block = flat[0].shape
    slots = sum(array.shape[0] for array in x[0])
    length, columns = q.shape
    width = sections * slots * block
    pair = 2 * DH
    pairs = columns // pair
    factor = DH ** (-0.5)

    def kernel(*refs):
        x_refs, refs = refs[:len(flat)], refs[len(flat):]
        (gain_ref, wk_ref, wv_ref, q_ref, g_ref, low_ref, grad_low_ref, keys_ref, values_ref,
         kg_ref, vg_ref, inverse_ref, extra_ref, memory_buf) = refs
        places = [(ref, i) for ref in x_refs for i in range(ref.shape[0])]

        def wide(j, i):
            ref, n = places[j * slots + i]
            return ref[n].astype(F32)

        squares = jnp.zeros((rows, block), F32)
        for j in range(sections):
            for i in range(slots):
                squares += wide(j, i) * wide(j, i)
        inverse = lax.rsqrt(jnp.sum(squares, axis=-1, keepdims=True) / width + EPSILON)
        inverse_ref[...] = jnp.broadcast_to(inverse, inverse_ref.shape)

        keys = jnp.zeros((rows, columns), F32)
        values = jnp.zeros((rows, columns), F32)
        for j in range(sections):
            for i in range(slots):
                row = first_row(direct, j, i, slots, block, TURN_GATHER, False)
                memory = wide(j, i) * inverse * gain_ref[row // block]
                memory_buf[pl.ds(row // block, 1)] = memory.astype(BF16)[None]
        for j in range(sections):
            blocks = [memory_buf[j * slots + i] for i in range(slots)]
            memory = jnp.concatenate(blocks, axis=1)
            span = slice(j * slots * block, (j + 1) * slots * block)
            keys += dot(memory, wk_ref[span, :])
            values += dot(memory, wv_ref[span, :])
        keys_ref[...] = keys.astype(BF16)
        values_ref[...] = values.astype(BF16)

        first = lax.broadcasted_iota(jnp.int32, (rows, pair), 1) < DH
        zero = jnp.zeros((rows, pair), BF16)
        c_sum = jnp.zeros((rows, pair), F32)
        for p in range(pairs):
            at = slice(p * pair, (p + 1) * pair)
            k, v = keys_ref[:, at], values_ref[:, at]
            q, g = q_ref[:, at], g_ref[:, at]
            k_two = jnp.concatenate((jnp.where(first, k, zero), jnp.where(first, zero, k)), axis=0)
            v_two = jnp.concatenate((jnp.where(first, v, zero), jnp.where(first, zero, v)), axis=0)
            scores = dot(k_two, q, NT)
            share_grad = dot(v_two, g, NT)
            for h in range(2):
                head = slice(h * rows, (h + 1) * rows)
                score = scores[head]
                raised = jnp.exp((score - jnp.max(score, axis=0, keepdims=True)) * factor)
                shares = raised * (1.0 / jnp.sum(raised, axis=0, keepdims=True))
                low_ref[p, head, :] = shares.astype(BF16)
                grads = share_grad[head]
                mean = jnp.sum(shares * grads, axis=0, keepdims=True)
                grad_low_ref[p, head, :] = (shares * (grads - mean) * factor).astype(BF16)
            vg = dot(low_ref[p], g)
            kg = dot(grad_low_ref[p], q)
            vg = jnp.where(first, vg[:rows], vg[rows:]).astype(BF16)
            kg = jnp.where(first, kg[:rows], kg[rows:]).astype(BF16)
            vg_ref[:, at] = vg
            kg_ref[:, at] = kg
            c_sum += kg.astype(F32) * k.astype(F32) + vg.astype(F32) * v.astype(F32)

        row = jnp.sum(c_sum.T, axis=0, keepdims=True)
        row = jnp.concatenate((row, jnp.zeros((1, EXTRA_WIDTH - rows), F32)), axis=1)
        high, low = split_rows(row)
        blank = jnp.zeros((EXTRA - 2, EXTRA_WIDTH), BF16)
        extra_ref[...] = jnp.concatenate((high, low, blank), axis=0)

    return pl.pallas_call(
        kernel,
        out_shape=(
            pltpu.VMEM((pairs, 2 * rows, length), BF16),
            pltpu.VMEM((pairs, 2 * rows, length), BF16),
            pltpu.VMEM((rows, columns), BF16),
            pltpu.VMEM((rows, columns), BF16),
            pltpu.VMEM((rows, columns), BF16),
            pltpu.VMEM((rows, columns), BF16),
            pltpu.VMEM((rows, 128), F32),
            pltpu.VMEM((EXTRA, EXTRA_WIDTH), BF16),
        ),
        in_specs=[VMEM] * (len(flat) + 5),
        out_specs=(VMEM,) * 8,
        scratch_shapes=[pltpu.VMEM((sections * slots, rows, block), BF16)],
        compiler_params=pltpu.CompilerParams(vmem_limit_bytes=16 << 20),
        cost_estimate=pl.CostEstimate(
            flops=4 * rows * width * columns + 16 * length * rows * columns,
            bytes_accessed=8 * width * columns,
            transcendentals=length * rows * columns // DH,
        ),
        name="attend",
    )(*flat, in_vmem(gain), in_vmem(wk), in_vmem(wv), q, g)


def mix(shares, weights):
    pairs, both, length = shares.shape
    rows, columns = weights.shape
    pair = columns // pairs

    def kernel(shares_ref, weights_ref, out_ref):
        first = lax.broadcasted_iota(jnp.int32, (rows, pair), 1) < DH
        zero = jnp.zeros((rows, pair), BF16)
        for p in range(pairs):
            at = slice(p * pair, (p + 1) * pair)
            w = weights_ref[:, at]
            two = jnp.concatenate((jnp.where(first, w, zero), jnp.where(first, zero, w)), axis=0)
            out_ref[:, at] = dot(two.T, shares_ref[p]).T.astype(BF16)

    return pl.pallas_call(
        kernel,
        out_shape=jax.ShapeDtypeStruct((length, columns), BF16),
        in_specs=[VMEM] * 2,
        out_specs=VMEM,
        compiler_params=pltpu.CompilerParams(vmem_limit_bytes=4 << 20),
        cost_estimate=cost(1, 1),
        name="mix",
    )(in_vmem(shares), in_vmem(weights))


def project(kg, vg, wk, wv, direct, j, slots, start, count, extra=None):
    rows, columns = kg.shape
    block = BLOCK
    tail = [] if extra is None else [in_vmem(extra)]
    more = 0 if extra is None else extra.shape[0]

    def kernel(kg_ref, vg_ref, wk_ref, wv_ref, *refs):
        kg, vg, out_ref = kg_ref[...], vg_ref[...], refs[-1]
        for i in range(count):
            span = pl.ds(first_row(direct, j, start + i, slots, block, TURN_SCATTER, REORDER), block)
            part = dot(kg, wk_ref[span, :], NT) + dot(vg, wv_ref[span, :], NT)
            out_ref[i * rows:(i + 1) * rows, :] = part.astype(BF16)
        if tail:
            out_ref[count * rows:, :] = refs[0][...]

    return pl.pallas_call(
        kernel,
        out_shape=pltpu.VMEM((count * rows + more, block), BF16),
        in_specs=[VMEM] * (4 + len(tail)),
        out_specs=VMEM,
        compiler_params=pltpu.CompilerParams(vmem_limit_bytes=4 << 20),
        cost_estimate=cost(1, 1),
        name="project",
    )(in_vmem(kg), in_vmem(vg), in_vmem(wk), in_vmem(wv), *tail)


def join(parts):
    def kernel(*refs):
        for n, ref in enumerate(refs[:-1]):
            refs[-1][n] = ref[0]

    return pl.pallas_call(
        kernel,
        out_shape=pltpu.VMEM((len(parts), *parts[0].shape[1:]), BF16),
        in_specs=[VMEM] * len(parts),
        out_specs=VMEM,
        compiler_params=pltpu.CompilerParams(vmem_limit_bytes=2 << 20),
        name="join",
    )(in_vmem(parts[0]), *parts[1:])


def total_of(refs, start, size):
    total = refs[0][start:start + size, :].astype(F32)
    for ref in refs[1:]:
        total += ref[start:start + size, :].astype(F32)
    return total


def sum_c(extra, c_rows):
    return extra[:c_rows] + extra[c_rows:2 * c_rows]


def c_tail(c):
    high, low = split_rows(c)
    blank = jnp.zeros((EXTRA - 2 * c.shape[0], c.shape[1]), BF16)
    return jnp.concatenate((high, low, blank), axis=0)


def sum_chunks(chunks, rows, c_rows):
    size, block = chunks[0].shape
    count = (size - EXTRA) // rows

    def kernel(*refs):
        parts, outs = refs[:len(chunks)], refs[len(chunks):]
        tail = c_tail(sum_c(total_of(parts, size - EXTRA, EXTRA), c_rows))
        outs[-1][...] = tail
        outs[0][...] = total_of(parts, 0, rows)
        for i in range(1, count):
            outs[i][:rows, :] = total_of(parts, i * rows, rows).astype(BF16)
            outs[i][rows:, :] = tail

    return pl.pallas_call(
        kernel,
        out_shape=(pltpu.VMEM((rows, block), F32),)
        + (pltpu.VMEM((rows + EXTRA, block), BF16),) * (count - 1)
        + (pltpu.VMEM((EXTRA, block), BF16),),
        in_specs=[VMEM] * len(chunks),
        out_specs=(VMEM,) * (count + 1),
        compiler_params=pltpu.CompilerParams(vmem_limit_bytes=4 << 20),
        name="sum_chunks",
    )(*chunks)


def gain_part(own_total, parts, hidden, inverse):
    rows, block = own_total.shape

    def kernel(hidden_ref, inverse_ref, own_ref, *refs):
        part_refs, out_ref = refs[:-1], refs[-1]
        total = own_ref[...] + total_of(part_refs, 0, rows)
        normed = hidden_ref[0].astype(F32) * inverse_ref[:, 0:1]
        out_ref[...] = jnp.sum(total * normed, axis=0, keepdims=True)

    return pl.pallas_call(
        kernel,
        out_shape=pltpu.VMEM((1, block), F32),
        in_specs=[VMEM] * (3 + len(parts)),
        out_specs=VMEM,
        compiler_params=pltpu.CompilerParams(vmem_limit_bytes=4 << 20),
        name="gain_part",
    )(in_vmem(hidden), in_vmem(inverse), in_vmem(own_total), *parts)


def finish(own_total, tail, parts, hidden, gain, inverse, width, c_rows, direct, slots):
    rows, block = own_total.shape

    def kernel(hidden_ref, gain_ref, inverse_ref, own_ref, tail_ref, *refs):
        part_refs, out_ref = refs[:-1], refs[-1]
        extra = tail_ref[...].astype(F32) + total_of(part_refs, rows, EXTRA)
        c = sum_c(extra, c_rows)
        c = jnp.concatenate([c[n:n + 1] for n in range(c_rows)], axis=1)[:, :rows]
        mean = (jnp.broadcast_to(c, (rows, rows)) / width).T[:, 0:1]
        total = own_ref[...] + total_of(part_refs, 0, rows)
        inverse = inverse_ref[:, 0:1]
        normed = hidden_ref[0].astype(F32) * inverse
        out_ref[...] = inverse * (total * gain_ref[first_row(direct, 0, 0, slots, 1, False, False)] - normed * mean)

    return pl.pallas_call(
        kernel,
        out_shape=jax.ShapeDtypeStruct((rows, block), F32),
        in_specs=[VMEM] * (5 + len(parts)),
        out_specs=VMEM,
        compiler_params=pltpu.CompilerParams(vmem_limit_bytes=4 << 20),
        cost_estimate=cost(0, 64 << 10),
        name="finish",
    )(in_vmem(hidden), in_vmem(gain), in_vmem(inverse), in_vmem(own_total), in_vmem(tail), *parts)


def add_gain(mine, theirs, replicas):
    def kernel(mine_ref, theirs_ref, out_ref):
        out_ref[...] = (mine_ref[...] + theirs_ref[...]) / replicas

    return pl.pallas_call(
        kernel,
        out_shape=jax.ShapeDtypeStruct(mine.shape, F32),
        in_specs=[VMEM, VMEM],
        out_specs=VMEM,
        compiler_params=pltpu.CompilerParams(vmem_limit_bytes=1 << 20),
        name="add_gain",
    )(in_vmem(mine), theirs)


def exchange(array, step, j, turned, reordered):
    names = ("section", "dp", "mp")
    sizes = [lax.axis_size(name) for name in names]
    pairs = []
    for n in range(math.prod(sizes)):
        section, core, mp = n // (sizes[1] * sizes[2]), n // sizes[2] % sizes[1], n % sizes[2]
        if (step == 2) != (turned and core % 2 == 1):
            section ^= j
        else:
            mp ^= far_first(j) if reordered else j
        pairs.append((n, (section * sizes[1] + core) * sizes[2] + mp))
    return lax.ppermute(array, names, pairs)


def swapped(array, axis, mine):
    return jnp.stack(
        [
            lax.dynamic_index_in_dim(array, jnp.bitwise_xor(mine, i), axis, False)
            for i in range(array.shape[axis])
        ],
        axis,
    )


def per_device(enc_hidden, enc_gain, key_weight, value_weight, queries, out_grad):
    own = enc_hidden[0]
    rows, own_columns = own.shape
    wk, wv = key_weight[0], value_weight[0]
    width, columns = wk.shape
    sections = lax.axis_size("section")
    groups = lax.axis_size("mp")
    replicas = lax.axis_size("dp")
    section = lax.axis_index("section")
    mp = lax.axis_index("mp")
    direct = own_columns == BLOCK and sections == groups
    c_rows = max(rows // own_columns, 1)

    slots = groups if direct else 4
    longest = sorted(range(1, max(sections, groups)), key=lambda j: (-bin(j).count("1"), -j))
    order = {1: [j for j in longest if j < groups], 2: [j for j in longest if j < sections]}

    def swap(step, array_of, turned, reordered):
        got = {j: exchange(array_of(j), step, j, direct and turned, direct and reordered) for j in order[step]}
        return [got[j] for j in sorted(got)]

    hidden, gain, wk, wv = fetch(
        own[None], enc_gain.reshape(width // BLOCK, 1, BLOCK), wk, wv
    )
    x = join([hidden] + swap(1, lambda j: own[None], TURN_GATHER, False))
    if direct:
        x = [(x,)] + [(part,) for part in swap(2, lambda j: x, TURN_GATHER, False)]
    else:
        x = lax.all_gather(x, "section", axis=0)
        x = swapped(x, 1, mp).transpose(2, 0, 1, 3).reshape(rows, -1, slots, BLOCK)
        x = [(part,) for part in x.transpose(1, 2, 0, 3)]
    low, grad_low, keys, values, kg, vg, inverse, extra = attend(
        x, gain, wk, wv, queries[0, 0], out_grad[0, 0], direct
    )

    if direct:
        own_gain = gain
        chunks = [
            project(kg, vg, wk, wv, direct, j, slots, 0, slots, extra) for j in range(sections)
        ]
    else:
        whole = [
            project(kg, vg, wk, wv, direct, n // slots, slots, n % slots, 1)
            for n in range(width // BLOCK)
        ]
        whole = jnp.stack(whole).transpose(1, 0, 2)
        whole = whole.reshape(rows, sections, groups, own_columns).transpose(1, 2, 0, 3)
        whole = swapped(swapped(whole, 1, mp), 0, section)
        tail = extra[:2, : c_rows * own_columns].reshape(2 * c_rows, own_columns)
        tail = jnp.concatenate((tail, jnp.zeros((EXTRA - 2 * c_rows, own_columns), BF16)))
        chunks = whole.reshape(sections, groups * rows, own_columns)
        chunks = [jnp.concatenate((part, tail)) for part in chunks]
        own_gain = lax.dynamic_slice_in_dim(
            enc_gain, (section * groups + mp) * own_columns, own_columns, 0
        ).reshape(1, 1, own_columns)

    attended, query_grad = mix(low, values), mix(grad_low, keys)
    got = swap(2, lambda j: chunks[j], TURN_SCATTER, REORDER)
    first, attended, query_grad = lax.optimization_barrier((chunks[0], attended, query_grad))
    own_total, *parts, tail = sum_chunks([first] + got, rows, c_rows)
    parts = swap(1, lambda j: parts[j - 1], TURN_SCATTER, REORDER)
    gain_own = gain_part(own_total, parts, hidden, inverse)
    if replicas == 2:
        gain_other = lax.ppermute(gain_own, "dp", [(0, 1), (1, 0)])
    else:
        gain_other = lax.psum(gain_own, "dp")
        gain_own = jnp.zeros_like(gain_own)
    hidden_grad = finish(own_total, tail, parts, hidden, own_gain, inverse, width, c_rows, direct, slots)
    gain_total = add_gain(gain_own, gain_other, replicas)
    return (
        attended[None, None],
        query_grad[None, None],
        hidden_grad[None],
        gain_total[0],
    )


def solution(mesh):
    in_specs = (
        P("dp", None, ("section", "mp")),
        P(),
        P("section", None, "mp"),
        P("section", None, "mp"),
        P("dp", "section", None, "mp"),
        P("dp", "section", None, "mp"),
    )
    out_specs = (
        P("dp", "section", None, "mp"),
        P("dp", "section", None, "mp"),
        P("dp", None, ("section", "mp")),
        P(("section", "mp")),
    )
    return jax.shard_map(
        per_device, mesh=mesh, in_specs=in_specs, out_specs=out_specs, check_vma=False
    )
```

```python
import math

import jax
import jax.numpy as jnp
from jax import lax
from jax.experimental import pallas as pl
from jax.experimental.pallas import tpu as pltpu
from jax.sharding import PartitionSpec as P

DH = 64
EPSILON = 1e-06
BLOCK = 256
EXTRA = 16
EXTRA_WIDTH = 256
PAD = 32
F32 = jnp.float32
BF16 = jnp.bfloat16
VMEM = pl.BlockSpec(memory_space=pltpu.VMEM)
SMEM = pl.BlockSpec(memory_space=pltpu.SMEM)
HBM = pl.BlockSpec(memory_space=pltpu.HBM)

NN = (((1,), (0,)), ((), ()))
NT = (((1,), (1,)), ((), ()))


def dot(a, b, dims=NN):
    return lax.dot_general(a, b, dims, preferred_element_type=F32)


def split_rows(row):
    high = row.astype(BF16)
    low = (row - high.astype(F32)).astype(BF16)
    return high, low


def in_vmem(array):
    return pltpu.with_memory_space_constraint(array, pltpu.VMEM)


def cost(flops, size):
    return pl.CostEstimate(flops=flops, bytes_accessed=size, transcendentals=0)


def in_hbm(array):
    return pltpu.with_memory_space_constraint(array, pltpu.HBM)


def block_at(direct, j, i, slots):
    if not direct:
        return j * slots + i
    section, mp, core = (lax.axis_index(name) for name in ("section", "mp", "dp"))
    turn = lax.rem(core, 2) * (i - j)
    return lax.bitwise_xor(section, j + turn) * slots + lax.bitwise_xor(mp, i - turn)


def fetch(hidden, gain, wk, wv, sections, slots, direct):
    width, columns = wk.shape
    block = width // (sections * slots)

    def kernel(*refs):
        ins, outs, few, many = refs[:4], refs[4:8], refs[8], refs[9]
        copies = [pltpu.make_async_copy(ins[n], outs[n], few.at[n]) for n in range(2)]
        for j in range(sections):
            for i in range(slots):
                row = pl.multiple_of(block_at(direct, j, i, slots) * block, block)
                n = j * slots + i
                copies += [
                    pltpu.make_async_copy(
                        ins[2 + w].at[pl.ds(row, block), :], outs[2 + w].at[n], many.at[w, n]
                    )
                    for w in range(2)
                ]
        for copy in copies:
            copy.start()
        for copy in copies:
            copy.wait()

    return pl.pallas_call(
        kernel,
        out_shape=(
            pltpu.VMEM(hidden.shape, BF16),
            pltpu.VMEM(gain.shape, F32),
            pltpu.VMEM((sections * slots, block, columns), BF16),
            pltpu.VMEM((sections * slots, block, columns), BF16),
        ),
        in_specs=[HBM] * 4,
        out_specs=(VMEM,) * 4,
        scratch_shapes=[
            pltpu.SemaphoreType.DMA((2,)), pltpu.SemaphoreType.DMA((2, sections * slots))
        ],
        compiler_params=pltpu.CompilerParams(vmem_limit_bytes=1 << 20),
        cost_estimate=cost(0, 8 * width * columns),
        name="fetch",
    )(*map(in_hbm, (hidden, gain, wk, wv)))


def attend(x, gain, wk, wv, q, g, direct):
    sections = len(x)
    flat = [array for arrays in x for array in arrays]
    _, rows, block = flat[0].shape
    slots = sum(array.shape[0] for array in x[0])
    length, columns = q.shape
    width = sections * slots * block
    pair = 2 * DH
    pairs = columns // pair
    factor = DH ** (-0.5)

    def kernel(*refs):
        x_refs, refs = refs[:len(flat)], refs[len(flat):]
        (gain_ref, wk_ref, wv_ref, q_ref, g_ref, low_ref, grad_low_ref, keys_ref, values_ref,
         kg_ref, vg_ref, inverse_ref, extra_ref, memory_buf) = refs
        places = [(ref, i) for ref in x_refs for i in range(ref.shape[0])]

        def wide(j, i):
            ref, n = places[j * slots + i]
            return ref[n].astype(F32)

        squares = jnp.zeros((rows, block), F32)
        for j in range(sections):
            for i in range(slots):
                squares += wide(j, i) * wide(j, i)
        inverse = lax.rsqrt(jnp.sum(squares, axis=-1, keepdims=True) / width + EPSILON)
        inverse_ref[...] = jnp.broadcast_to(inverse, inverse_ref.shape)

        keys = jnp.zeros((rows, columns), F32)
        values = jnp.zeros((rows, columns), F32)
        for j in range(sections):
            for i in range(slots):
                memory = wide(j, i) * inverse * gain_ref[block_at(direct, j, i, slots)]
                memory_buf[:, i * block:(i + 1) * block] = memory.astype(BF16)
            span = slice(j * slots, (j + 1) * slots)
            keys += dot(memory_buf[...], wk_ref[span].reshape(slots * block, columns))
            values += dot(memory_buf[...], wv_ref[span].reshape(slots * block, columns))
        keys_ref[...] = keys.astype(BF16)
        values_ref[...] = values.astype(BF16)

        first = lax.broadcasted_iota(jnp.int32, (rows, pair), 1) < DH
        zero = jnp.zeros((rows, pair), BF16)
        c_sum = jnp.zeros((rows, pair), F32)
        for p in range(pairs):
            at = slice(p * pair, (p + 1) * pair)
            k, v = keys_ref[:, at], values_ref[:, at]
            q, g = q_ref[:, at], g_ref[:, at]
            k_two = jnp.concatenate((jnp.where(first, k, zero), jnp.where(first, zero, k)), axis=0)
            v_two = jnp.concatenate((jnp.where(first, v, zero), jnp.where(first, zero, v)), axis=0)
            scores = dot(k_two, q, NT)
            share_grad = dot(v_two, g, NT)
            for h in range(2):
                head = slice(h * rows, (h + 1) * rows)
                score = scores[head]
                raised = jnp.exp((score - jnp.max(score, axis=0, keepdims=True)) * factor)
                shares = raised * (1.0 / jnp.sum(raised, axis=0, keepdims=True))
                low_ref[p, head, :] = shares.astype(BF16)
                grads = share_grad[head]
                mean = jnp.sum(shares * grads, axis=0, keepdims=True)
                grad_low_ref[p, head, :] = (shares * (grads - mean) * factor).astype(BF16)
            vg = dot(low_ref[p], g)
            kg = dot(grad_low_ref[p], q)
            vg = jnp.where(first, vg[:rows], vg[rows:]).astype(BF16)
            kg = jnp.where(first, kg[:rows], kg[rows:]).astype(BF16)
            vg_ref[:, at] = vg
            kg_ref[:, at] = kg
            c_sum += kg.astype(F32) * k.astype(F32) + vg.astype(F32) * v.astype(F32)

        row = jnp.sum(c_sum.T, axis=0, keepdims=True)
        row = jnp.concatenate((row, jnp.zeros((1, EXTRA_WIDTH - rows), F32)), axis=1)
        high, low = split_rows(row)
        blank = jnp.zeros((EXTRA - 2, EXTRA_WIDTH), BF16)
        extra_ref[...] = jnp.concatenate((high, low, blank), axis=0)

    return pl.pallas_call(
        kernel,
        out_shape=(
            pltpu.VMEM((pairs, 2 * rows, length), BF16),
            pltpu.VMEM((pairs, 2 * rows, length), BF16),
            pltpu.VMEM((rows, columns), BF16),
            pltpu.VMEM((rows, columns), BF16),
            pltpu.VMEM((rows, columns), BF16),
            pltpu.VMEM((rows, columns), BF16),
            pltpu.VMEM((rows, 128), F32),
            pltpu.VMEM((EXTRA, EXTRA_WIDTH), BF16),
        ),
        in_specs=[VMEM] * (len(flat) + 5),
        out_specs=(VMEM,) * 8,
        scratch_shapes=[pltpu.VMEM((rows, slots * block), BF16)],
        compiler_params=pltpu.CompilerParams(vmem_limit_bytes=16 << 20),
        cost_estimate=pl.CostEstimate(
            flops=4 * rows * width * columns + 16 * length * rows * columns,
            bytes_accessed=8 * width * columns,
            transcendentals=length * rows * columns // DH,
        ),
        name="attend",
    )(*flat, in_vmem(gain), in_vmem(wk), in_vmem(wv), q, g)


def mix(shares, weights):
    pairs, both, length = shares.shape
    rows, columns = weights.shape
    pair = columns // pairs

    def kernel(shares_ref, weights_ref, out_ref):
        first = lax.broadcasted_iota(jnp.int32, (rows, pair), 1) < DH
        zero = jnp.zeros((rows, pair), BF16)
        for p in range(pairs):
            at = slice(p * pair, (p + 1) * pair)
            w = weights_ref[:, at]
            two = jnp.concatenate((jnp.where(first, w, zero), jnp.where(first, zero, w)), axis=0)
            out_ref[:, at] = dot(two.T, shares_ref[p]).T.astype(BF16)

    return pl.pallas_call(
        kernel,
        out_shape=jax.ShapeDtypeStruct((length, columns), BF16),
        in_specs=[VMEM] * 2,
        out_specs=VMEM,
        compiler_params=pltpu.CompilerParams(vmem_limit_bytes=4 << 20),
        cost_estimate=cost(1, 1),
        name="mix",
    )(in_vmem(shares), in_vmem(weights))


def project(kg, vg, wk, wv, start, count, extra=None, size=0):
    rows, columns = kg.shape
    block = wk.shape[1]
    tail = [] if extra is None else [in_vmem(extra)]
    end = count * rows + EXTRA * len(tail)
    size = max(size, end)

    def kernel(kg_ref, vg_ref, wk_ref, wv_ref, *refs):
        kg, vg, out_ref = kg_ref[...], vg_ref[...], refs[-1]
        for i in range(count):
            part = dot(kg, wk_ref[start + i], NT) + dot(vg, wv_ref[start + i], NT)
            out_ref[i * rows:(i + 1) * rows, :] = part.astype(BF16)
        if tail:
            out_ref[count * rows:end, :] = refs[0][...]
        if size > end:
            out_ref[end:, :] = jnp.zeros((size - end, block), BF16)

    return pl.pallas_call(
        kernel,
        out_shape=pltpu.VMEM((size, block), BF16),
        in_specs=[VMEM] * (4 + len(tail)),
        out_specs=VMEM,
        compiler_params=pltpu.CompilerParams(vmem_limit_bytes=4 << 20),
        cost_estimate=cost(1, 1),
        name="project",
    )(in_vmem(kg), in_vmem(vg), in_vmem(wk), in_vmem(wv), *tail)


def join(parts):
    def kernel(*refs):
        for n, ref in enumerate(refs[:-1]):
            refs[-1][n] = ref[0]

    return pl.pallas_call(
        kernel,
        out_shape=pltpu.VMEM((len(parts), *parts[0].shape[1:]), BF16),
        in_specs=[VMEM] * len(parts),
        out_specs=VMEM,
        compiler_params=pltpu.CompilerParams(vmem_limit_bytes=2 << 20),
        name="join",
    )(in_vmem(parts[0]), *parts[1:])


def total_of(refs, start, size):
    total = refs[0][start:start + size, :].astype(F32)
    for ref in refs[1:]:
        total += ref[start:start + size, :].astype(F32)
    return total


def sum_c(extra, c_rows):
    return extra[:c_rows] + extra[c_rows:2 * c_rows]


def c_tail(c):
    high, low = split_rows(c)
    blank = jnp.zeros((EXTRA - 2 * c.shape[0], c.shape[1]), BF16)
    return jnp.concatenate((high, low, blank), axis=0)


def sum_chunks(chunks, count, rows, c_rows):
    block = chunks[0].shape[1]

    def kernel(*refs):
        parts, outs = refs[:len(chunks)], refs[len(chunks):]
        tail = c_tail(sum_c(total_of(parts, count * rows, EXTRA), c_rows))
        outs[-1][...] = tail
        outs[0][...] = total_of(parts, 0, rows)
        for i in range(1, count):
            outs[i][:rows, :] = total_of(parts, i * rows, rows).astype(BF16)
            outs[i][rows:, :] = tail

    return pl.pallas_call(
        kernel,
        out_shape=(pltpu.VMEM((rows, block), F32),)
        + (pltpu.VMEM((rows + EXTRA, block), BF16),) * (count - 1)
        + (pltpu.VMEM((EXTRA, block), BF16),),
        in_specs=[VMEM] * len(chunks),
        out_specs=(VMEM,) * (count + 1),
        compiler_params=pltpu.CompilerParams(vmem_limit_bytes=4 << 20),
        name="sum_chunks",
    )(*chunks)


def gain_part(own_total, parts, hidden, inverse):
    rows, block = own_total.shape

    def kernel(hidden_ref, inverse_ref, own_ref, *refs):
        part_refs, out_ref = refs[:-1], refs[-1]
        total = own_ref[...] + total_of(part_refs, 0, rows)
        normed = hidden_ref[0].astype(F32) * inverse_ref[:, 0:1]
        out_ref[...] = jnp.sum(total * normed, axis=0, keepdims=True)

    return pl.pallas_call(
        kernel,
        out_shape=pltpu.VMEM((1, block), F32),
        in_specs=[VMEM] * (3 + len(parts)),
        out_specs=VMEM,
        compiler_params=pltpu.CompilerParams(vmem_limit_bytes=4 << 20),
        name="gain_part",
    )(in_vmem(hidden), in_vmem(inverse), in_vmem(own_total), *parts)


def finish(own_total, tail, parts, hidden, gain, inverse, width, c_rows, direct, slots):
    rows, block = own_total.shape

    def kernel(hidden_ref, gain_ref, inverse_ref, own_ref, tail_ref, *refs):
        part_refs, out_ref = refs[:-1], refs[-1]
        extra = tail_ref[...].astype(F32) + total_of(part_refs, rows, EXTRA)
        c = sum_c(extra, c_rows)
        c = jnp.concatenate([c[n:n + 1] for n in range(c_rows)], axis=1)[:, :rows]
        mean = (jnp.broadcast_to(c, (rows, rows)) / width).T[:, 0:1]
        total = own_ref[...] + total_of(part_refs, 0, rows)
        inverse = inverse_ref[:, 0:1]
        normed = hidden_ref[0].astype(F32) * inverse
        out_ref[...] = inverse * (total * gain_ref[block_at(direct, 0, 0, slots)] - normed * mean)

    return pl.pallas_call(
        kernel,
        out_shape=jax.ShapeDtypeStruct((rows, block), F32),
        in_specs=[VMEM] * (5 + len(parts)),
        out_specs=VMEM,
        compiler_params=pltpu.CompilerParams(vmem_limit_bytes=4 << 20),
        cost_estimate=cost(0, 64 << 10),
        name="finish",
    )(in_vmem(hidden), in_vmem(gain), in_vmem(inverse), in_vmem(own_total), in_vmem(tail), *parts)


def add_gain(mine, theirs, replicas):
    def kernel(mine_ref, theirs_ref, out_ref):
        out_ref[...] = (mine_ref[...] + theirs_ref[...]) / replicas

    return pl.pallas_call(
        kernel,
        out_shape=jax.ShapeDtypeStruct(mine.shape, F32),
        in_specs=[VMEM, VMEM],
        out_specs=VMEM,
        compiler_params=pltpu.CompilerParams(vmem_limit_bytes=1 << 20),
        name="add_gain",
    )(in_vmem(mine), theirs)


def exchange(array, step, j, direct):
    names = ("section", "dp", "mp")
    sizes = [lax.axis_size(name) for name in names]
    pairs = []
    for n in range(math.prod(sizes)):
        section, core, mp = n // (sizes[1] * sizes[2]), n // sizes[2] % sizes[1], n % sizes[2]
        if (step == 2) != (direct and core % 2 == 1):
            section ^= j
        else:
            mp ^= j
        pairs.append((n, (section * sizes[1] + core) * sizes[2] + mp))
    return lax.ppermute(array, names, pairs)


def swapped(array, axis, mine):
    return jnp.stack(
        [
            lax.dynamic_index_in_dim(array, jnp.bitwise_xor(mine, i), axis, False)
            for i in range(array.shape[axis])
        ],
        axis,
    )


def per_device(enc_hidden, enc_gain, key_weight, value_weight, queries, out_grad):
    own = enc_hidden[0]
    rows, own_columns = own.shape
    wk, wv = key_weight[0], value_weight[0]
    width, columns = wk.shape
    sections = lax.axis_size("section")
    groups = lax.axis_size("mp")
    replicas = lax.axis_size("dp")
    section = lax.axis_index("section")
    mp = lax.axis_index("mp")
    direct = own_columns == BLOCK and sections == groups
    c_rows = max(rows // own_columns, 1)

    slots = groups if direct else 4

    def swap(step, arrays):
        got = [exchange(array, step, j, direct) for j, array in enumerate(arrays) if j]
        return [arrays[0]] + got

    gain = enc_gain.reshape(width // BLOCK, 1, BLOCK)
    parts = width // (slots * BLOCK)
    hidden, gain, wk, wv = fetch(own[None], gain, wk, wv, parts, slots, direct)
    x = join([hidden] + swap(1, [own[None]] * groups)[1:])
    if direct:
        x = [(part,) for part in swap(2, [x] * sections)]
    else:
        x = lax.all_gather(x, "section", axis=0)
        x = swapped(x, 1, mp).transpose(2, 0, 1, 3).reshape(rows, -1, slots, BLOCK)
        x = [(part,) for part in x.transpose(1, 2, 0, 3)]
    low, grad_low, keys, values, kg, vg, inverse, extra = attend(
        x, gain, wk, wv, queries[0, 0], out_grad[0, 0], direct
    )

    if direct:
        own_gain = gain
        size = {sections - 1: slots * rows + EXTRA + PAD}
        chunks = {
            j: project(kg, vg, wk, wv, j * slots, slots, extra, size.get(j, 0))
            for j in (0, *range(sections - 1, 0, -1))
        }
        chunks = [chunks[j] for j in range(sections)]
    else:
        whole = [
            project(kg, vg, wk, wv, n, 1) for n in range(width // BLOCK)
        ]
        whole = jnp.stack(whole).transpose(1, 0, 2)
        whole = whole.reshape(rows, sections, groups, own_columns).transpose(1, 2, 0, 3)
        whole = swapped(swapped(whole, 1, mp), 0, section)
        tail = extra[:2, : c_rows * own_columns].reshape(2 * c_rows, own_columns)
        tail = jnp.concatenate((tail, jnp.zeros((EXTRA - 2 * c_rows, own_columns), BF16)))
        chunks = whole.reshape(sections, groups * rows, own_columns)
        chunks = [jnp.concatenate((part, tail)) for part in chunks]
        own_gain = lax.dynamic_slice_in_dim(
            enc_gain, (section * groups + mp) * own_columns, own_columns, 0
        ).reshape(1, 1, own_columns)

    attended, query_grad = mix(low, values), mix(grad_low, keys)
    first, *got = swap(2, chunks)
    first, attended, query_grad = lax.optimization_barrier((first, attended, query_grad))
    own_total, *parts, tail = sum_chunks([first] + got[::-1], groups, rows, c_rows)
    parts = swap(1, [own_total] + parts)[:0:-1]
    gain_own = gain_part(own_total, parts, hidden, inverse)
    if replicas == 2:
        gain_other = lax.ppermute(gain_own, "dp", [(0, 1), (1, 0)])
    else:
        gain_other = lax.psum(gain_own, "dp")
        gain_own = jnp.zeros_like(gain_own)
    hidden_grad = finish(own_total, tail, parts, hidden, own_gain, inverse, width, c_rows, direct, slots)
    gain_total = add_gain(gain_own, gain_other, replicas)
    return (
        attended[None, None],
        query_grad[None, None],
        hidden_grad[None],
        gain_total[0],
    )


def solution(mesh):
    in_specs = (
        P("dp", None, ("section", "mp")),
        P(),
        P("section", None, "mp"),
        P("section", None, "mp"),
        P("dp", "section", None, "mp"),
        P("dp", "section", None, "mp"),
    )
    out_specs = (
        P("dp", "section", None, "mp"),
        P("dp", "section", None, "mp"),
        P("dp", None, ("section", "mp")),
        P(("section", "mp")),
    )
    return jax.shard_map(
        per_device, mesh=mesh, in_specs=in_specs, out_specs=out_specs, check_vma=False
    )
```

```python
import math

import jax
import jax.numpy as jnp
from jax import lax
from jax.experimental import pallas as pl
from jax.experimental.pallas import tpu as pltpu
from jax.sharding import PartitionSpec as P

DH = 64
EPSILON = 1e-06
BLOCK = 256
EXTRA = 16
EXTRA_WIDTH = 256
PAD = 16
F32 = jnp.float32
BF16 = jnp.bfloat16
VMEM = pl.BlockSpec(memory_space=pltpu.VMEM)
SMEM = pl.BlockSpec(memory_space=pltpu.SMEM)
HBM = pl.BlockSpec(memory_space=pltpu.HBM)

NN = (((1,), (0,)), ((), ()))
NT = (((1,), (1,)), ((), ()))


def dot(a, b, dims=NN):
    return lax.dot_general(a, b, dims, preferred_element_type=F32)


def split_rows(row):
    high = row.astype(BF16)
    low = (row - high.astype(F32)).astype(BF16)
    return high, low


def in_vmem(array):
    return pltpu.with_memory_space_constraint(array, pltpu.VMEM)


def cost(flops, size):
    return pl.CostEstimate(flops=flops, bytes_accessed=size, transcendentals=0)


def in_hbm(array):
    return pltpu.with_memory_space_constraint(array, pltpu.HBM)


def block_at(direct, j, i, slots):
    if not direct:
        return j * slots + i
    section, mp, core = (lax.axis_index(name) for name in ("section", "mp", "dp"))
    turn = lax.rem(core, 2) * (i - j)
    return lax.bitwise_xor(section, j + turn) * slots + lax.bitwise_xor(mp, i - turn)


def fetch(arrays, weights, sections, slots, direct):
    width, columns = weights[0].shape
    block = width // (sections * slots)
    few, many = len(arrays), len(weights)

    def kernel(*refs):
        ins, outs, sems = refs[:few + many], refs[few + many:-1], refs[-1]
        copies = [pltpu.make_async_copy(ins[n], outs[n], sems.at[many, n]) for n in range(few)]
        for j in range(sections):
            for i in range(slots):
                row = pl.multiple_of(block_at(direct, j, i, slots) * block, block)
                n = j * slots + i
                copies += [
                    pltpu.make_async_copy(
                        ins[few + w].at[pl.ds(row, block), :], outs[few + w].at[n], sems.at[w, n]
                    )
                    for w in range(many)
                ]
        for copy in copies:
            copy.start()
        for copy in copies:
            copy.wait()

    return pl.pallas_call(
        kernel,
        out_shape=tuple(pltpu.VMEM(array.shape, array.dtype) for array in arrays)
        + (pltpu.VMEM((sections * slots, block, columns), BF16),) * many,
        in_specs=[HBM] * (few + many),
        out_specs=(VMEM,) * (few + many),
        scratch_shapes=[pltpu.SemaphoreType.DMA((many + 1, sections * slots))],
        compiler_params=pltpu.CompilerParams(vmem_limit_bytes=1 << 20),
        cost_estimate=cost(0, 4 * many * width * columns),
        name="fetch",
    )(*map(in_hbm, (*arrays, *weights)))


def attend(x, gain, wk, wv, q, g, direct):
    sections = len(x)
    flat = [array for arrays in x for array in arrays]
    _, rows, block = flat[0].shape
    slots = sum(array.shape[0] for array in x[0])
    length, columns = q.shape
    width = sections * slots * block
    pair = 2 * DH
    pairs = columns // pair
    factor = DH ** (-0.5)

    def kernel(*refs):
        x_refs, refs = refs[:len(flat)], refs[len(flat):]
        (gain_ref, wk_ref, wv_ref, q_ref, g_ref, low_ref, grad_low_ref, keys_ref, values_ref,
         kg_ref, vg_ref, inverse_ref, extra_ref, memory_buf) = refs
        places = [(ref, i) for ref in x_refs for i in range(ref.shape[0])]

        def wide(j, i):
            ref, n = places[j * slots + i]
            return ref[n].astype(F32)

        squares = jnp.zeros((rows, block), F32)
        for j in range(sections):
            for i in range(slots):
                squares += wide(j, i) * wide(j, i)
        inverse = lax.rsqrt(jnp.sum(squares, axis=-1, keepdims=True) / width + EPSILON)
        inverse_ref[...] = jnp.broadcast_to(inverse, inverse_ref.shape)

        keys = jnp.zeros((rows, columns), F32)
        values = jnp.zeros((rows, columns), F32)
        for j in range(sections):
            for i in range(slots):
                memory = wide(j, i) * inverse * gain_ref[block_at(direct, j, i, slots)]
                memory_buf[:, i * block:(i + 1) * block] = memory.astype(BF16)
            span = slice(j * slots, (j + 1) * slots)
            keys += dot(memory_buf[...], wk_ref[span].reshape(slots * block, columns))
            values += dot(memory_buf[...], wv_ref[span].reshape(slots * block, columns))
        keys_ref[...] = keys.astype(BF16)
        values_ref[...] = values.astype(BF16)

        first = lax.broadcasted_iota(jnp.int32, (rows, pair), 1) < DH
        zero = jnp.zeros((rows, pair), BF16)
        c_sum = jnp.zeros((rows, pair), F32)
        for p in range(pairs):
            at = slice(p * pair, (p + 1) * pair)
            k, v = keys_ref[:, at], values_ref[:, at]
            q, g = q_ref[:, at], g_ref[:, at]
            k_two = jnp.concatenate((jnp.where(first, k, zero), jnp.where(first, zero, k)), axis=0)
            v_two = jnp.concatenate((jnp.where(first, v, zero), jnp.where(first, zero, v)), axis=0)
            scores = dot(k_two, q, NT)
            share_grad = dot(v_two, g, NT)
            for h in range(2):
                head = slice(h * rows, (h + 1) * rows)
                score = scores[head]
                raised = jnp.exp((score - jnp.max(score, axis=0, keepdims=True)) * factor)
                shares = raised * (1.0 / jnp.sum(raised, axis=0, keepdims=True))
                low_ref[p, head, :] = shares.astype(BF16)
                grads = share_grad[head]
                mean = jnp.sum(shares * grads, axis=0, keepdims=True)
                grad_low_ref[p, head, :] = (shares * (grads - mean) * factor).astype(BF16)
            vg = dot(low_ref[p], g)
            kg = dot(grad_low_ref[p], q)
            vg = jnp.where(first, vg[:rows], vg[rows:]).astype(BF16)
            kg = jnp.where(first, kg[:rows], kg[rows:]).astype(BF16)
            vg_ref[:, at] = vg
            kg_ref[:, at] = kg
            c_sum += kg.astype(F32) * k.astype(F32) + vg.astype(F32) * v.astype(F32)

        row = jnp.sum(c_sum.T, axis=0, keepdims=True)
        row = jnp.concatenate((row, jnp.zeros((1, EXTRA_WIDTH - rows), F32)), axis=1)
        high, low = split_rows(row)
        blank = jnp.zeros((EXTRA - 2, EXTRA_WIDTH), BF16)
        extra_ref[...] = jnp.concatenate((high, low, blank), axis=0)

    return pl.pallas_call(
        kernel,
        out_shape=(
            pltpu.VMEM((pairs, 2 * rows, length), BF16),
            pltpu.VMEM((pairs, 2 * rows, length), BF16),
            pltpu.VMEM((rows, columns), BF16),
            pltpu.VMEM((rows, columns), BF16),
            pltpu.VMEM((rows, columns), BF16),
            pltpu.VMEM((rows, columns), BF16),
            pltpu.VMEM((rows, 128), F32),
            pltpu.VMEM((EXTRA, EXTRA_WIDTH), BF16),
        ),
        in_specs=[VMEM] * (len(flat) + 5),
        out_specs=(VMEM,) * 8,
        scratch_shapes=[pltpu.VMEM((rows, slots * block), BF16)],
        compiler_params=pltpu.CompilerParams(vmem_limit_bytes=16 << 20),
        cost_estimate=pl.CostEstimate(
            flops=4 * rows * width * columns + 16 * length * rows * columns,
            bytes_accessed=8 * width * columns,
            transcendentals=length * rows * columns // DH,
        ),
        name="attend",
    )(*flat, in_vmem(gain), in_vmem(wk), in_vmem(wv), q, g)


def mix(shares, weights):
    pairs, both, length = shares.shape
    rows, columns = weights.shape
    pair = columns // pairs

    def kernel(shares_ref, weights_ref, out_ref):
        first = lax.broadcasted_iota(jnp.int32, (rows, pair), 1) < DH
        zero = jnp.zeros((rows, pair), BF16)
        for p in range(pairs):
            at = slice(p * pair, (p + 1) * pair)
            w = weights_ref[:, at]
            two = jnp.concatenate((jnp.where(first, w, zero), jnp.where(first, zero, w)), axis=0)
            out_ref[:, at] = dot(two.T, shares_ref[p]).T.astype(BF16)

    return pl.pallas_call(
        kernel,
        out_shape=jax.ShapeDtypeStruct((length, columns), BF16),
        in_specs=[VMEM] * 2,
        out_specs=VMEM,
        compiler_params=pltpu.CompilerParams(vmem_limit_bytes=4 << 20),
        cost_estimate=cost(1, 1),
        name="mix",
    )(in_vmem(shares), in_vmem(weights))


def project(kg, vg, wk, wv, start, count, extra=None, size=0):
    rows, columns = kg.shape
    block = wk.shape[1]
    tail = [] if extra is None else [in_vmem(extra)]
    end = count * rows + EXTRA * len(tail)
    size = max(size, end)

    def kernel(kg_ref, vg_ref, wk_ref, wv_ref, *refs):
        kg, vg, out_ref = kg_ref[...], vg_ref[...], refs[-1]
        for i in range(count):
            part = dot(kg, wk_ref[start + i], NT) + dot(vg, wv_ref[start + i], NT)
            out_ref[i * rows:(i + 1) * rows, :] = part.astype(BF16)
        if tail:
            out_ref[count * rows:end, :] = refs[0][...]
        if size > end:
            out_ref[end:, :] = jnp.zeros((size - end, block), BF16)

    return pl.pallas_call(
        kernel,
        out_shape=pltpu.VMEM((size, block), BF16),
        in_specs=[VMEM] * (4 + len(tail)),
        out_specs=VMEM,
        compiler_params=pltpu.CompilerParams(vmem_limit_bytes=4 << 20),
        cost_estimate=cost(1, 1),
        name="project",
    )(in_vmem(kg), in_vmem(vg), in_vmem(wk), in_vmem(wv), *tail)


def join(parts, order):
    def kernel(*refs):
        for n, ref in zip(order, refs[:-1]):
            refs[-1][n] = ref[0]

    return pl.pallas_call(
        kernel,
        out_shape=pltpu.VMEM((len(parts), *parts[0].shape[1:]), BF16),
        in_specs=[VMEM] * len(parts),
        out_specs=VMEM,
        compiler_params=pltpu.CompilerParams(vmem_limit_bytes=2 << 20),
        name="join",
    )(in_vmem(parts[0]), *parts[1:])


def total_of(refs, start, size):
    total = refs[0][start:start + size, :].astype(F32)
    for ref in refs[1:]:
        total += ref[start:start + size, :].astype(F32)
    return total


def sum_c(extra, c_rows):
    return extra[:c_rows] + extra[c_rows:2 * c_rows]


def c_tail(c):
    high, low = split_rows(c)
    blank = jnp.zeros((EXTRA - 2 * c.shape[0], c.shape[1]), BF16)
    return jnp.concatenate((high, low, blank), axis=0)


def sum_chunks(chunks, count, rows, c_rows):
    block = chunks[0].shape[1]

    def kernel(*refs):
        parts, outs = refs[:len(chunks)], refs[len(chunks):]
        tail = c_tail(sum_c(total_of(parts, count * rows, EXTRA), c_rows))
        outs[-1][...] = tail
        outs[0][...] = total_of(parts, 0, rows)
        for i in range(1, count):
            outs[i][:rows, :] = total_of(parts, i * rows, rows).astype(BF16)
            outs[i][rows:, :] = tail

    return pl.pallas_call(
        kernel,
        out_shape=(pltpu.VMEM((rows, block), F32),)
        + (pltpu.VMEM((rows + EXTRA, block), BF16),) * (count - 1)
        + (pltpu.VMEM((EXTRA, block), BF16),),
        in_specs=[VMEM] * len(chunks),
        out_specs=(VMEM,) * (count + 1),
        compiler_params=pltpu.CompilerParams(vmem_limit_bytes=4 << 20),
        name="sum_chunks",
    )(*chunks)


def gain_part(own_total, parts, hidden, inverse):
    rows, block = own_total.shape

    def kernel(hidden_ref, inverse_ref, own_ref, *refs):
        part_refs, out_ref = refs[:-1], refs[-1]
        total = own_ref[...] + total_of(part_refs, 0, rows)
        normed = hidden_ref[0].astype(F32) * inverse_ref[:, 0:1]
        out_ref[...] = jnp.sum(total * normed, axis=0, keepdims=True)

    return pl.pallas_call(
        kernel,
        out_shape=pltpu.VMEM((1, block), F32),
        in_specs=[VMEM] * (3 + len(parts)),
        out_specs=VMEM,
        compiler_params=pltpu.CompilerParams(vmem_limit_bytes=4 << 20),
        name="gain_part",
    )(in_vmem(hidden), in_vmem(inverse), in_vmem(own_total), *parts)


def finish(own_total, tail, parts, hidden, gain, inverse, width, c_rows, direct, slots):
    rows, block = own_total.shape

    def kernel(hidden_ref, gain_ref, inverse_ref, own_ref, tail_ref, *refs):
        part_refs, out_ref = refs[:-1], refs[-1]
        extra = tail_ref[...].astype(F32) + total_of(part_refs, rows, EXTRA)
        c = sum_c(extra, c_rows)
        c = jnp.concatenate([c[n:n + 1] for n in range(c_rows)], axis=1)[:, :rows]
        mean = (jnp.broadcast_to(c, (rows, rows)) / width).T[:, 0:1]
        total = own_ref[...] + total_of(part_refs, 0, rows)
        inverse = inverse_ref[:, 0:1]
        normed = hidden_ref[0].astype(F32) * inverse
        out_ref[...] = inverse * (total * gain_ref[block_at(direct, 0, 0, slots)] - normed * mean)

    return pl.pallas_call(
        kernel,
        out_shape=jax.ShapeDtypeStruct((rows, block), F32),
        in_specs=[VMEM] * (5 + len(parts)),
        out_specs=VMEM,
        compiler_params=pltpu.CompilerParams(vmem_limit_bytes=4 << 20),
        cost_estimate=cost(0, 64 << 10),
        name="finish",
    )(in_vmem(hidden), in_vmem(gain), in_vmem(inverse), in_vmem(own_total), in_vmem(tail), *parts)


def add_gain(mine, theirs, replicas):
    def kernel(mine_ref, theirs_ref, out_ref):
        out_ref[...] = (mine_ref[...] + theirs_ref[...]) / replicas

    return pl.pallas_call(
        kernel,
        out_shape=jax.ShapeDtypeStruct(mine.shape, F32),
        in_specs=[VMEM, VMEM],
        out_specs=VMEM,
        compiler_params=pltpu.CompilerParams(vmem_limit_bytes=1 << 20),
        name="add_gain",
    )(in_vmem(mine), theirs)


def exchange(array, step, j, direct):
    names = ("section", "dp", "mp")
    sizes = [lax.axis_size(name) for name in names]
    pairs = []
    for n in range(math.prod(sizes)):
        section, core, mp = n // (sizes[1] * sizes[2]), n // sizes[2] % sizes[1], n % sizes[2]
        if (step == 2) != (direct and core % 2 == 1):
            section ^= j
        else:
            mp ^= j
        pairs.append((n, (section * sizes[1] + core) * sizes[2] + mp))
    return lax.ppermute(array, names, pairs)


def swapped(array, axis, mine):
    return jnp.stack(
        [
            lax.dynamic_index_in_dim(array, jnp.bitwise_xor(mine, i), axis, False)
            for i in range(array.shape[axis])
        ],
        axis,
    )


def per_device(enc_hidden, enc_gain, key_weight, value_weight, queries, out_grad):
    own = enc_hidden[0]
    rows, own_columns = own.shape
    wk, wv = key_weight[0], value_weight[0]
    width, columns = wk.shape
    sections = lax.axis_size("section")
    groups = lax.axis_size("mp")
    replicas = lax.axis_size("dp")
    section = lax.axis_index("section")
    mp = lax.axis_index("mp")
    direct = own_columns == BLOCK and sections == groups
    c_rows = max(rows // own_columns, 1)

    slots = groups if direct else 4

    def swap(step, arrays):
        got = [exchange(array, step, j, direct) for j, array in enumerate(arrays) if j]
        return [arrays[0]] + got

    gain = enc_gain.reshape(width // BLOCK, 1, BLOCK)
    parts = width // (slots * BLOCK)
    hidden, gain, wk = fetch((own[None], gain), (wk,), parts, slots, direct)
    (wv,) = fetch((), (wv,), parts, slots, direct)
    column = [hidden] + swap(1, [own[None]] * groups)[1:]
    order = sorted(range(groups), key=lambda j: (j > 0, j != 3, j))
    x = join([column[j] for j in order], order)
    if direct:
        x = [(part,) for part in swap(2, [x] * sections)]
    else:
        x = lax.all_gather(x, "section", axis=0)
        x = swapped(x, 1, mp).transpose(2, 0, 1, 3).reshape(rows, -1, slots, BLOCK)
        x = [(part,) for part in x.transpose(1, 2, 0, 3)]
    low, grad_low, keys, values, kg, vg, inverse, extra = attend(
        x, gain, wk, wv, queries[0, 0], out_grad[0, 0], direct
    )

    if direct:
        own_gain = gain
        size = {sections - 1: slots * rows + EXTRA + PAD}
        chunks = {
            j: project(kg, vg, wk, wv, j * slots, slots, extra, size.get(j, 0))
            for j in (0, *range(sections - 1, 0, -1))
        }
        chunks = [chunks[j] for j in range(sections)]
    else:
        whole = [
            project(kg, vg, wk, wv, n, 1) for n in range(width // BLOCK)
        ]
        whole = jnp.stack(whole).transpose(1, 0, 2)
        whole = whole.reshape(rows, sections, groups, own_columns).transpose(1, 2, 0, 3)
        whole = swapped(swapped(whole, 1, mp), 0, section)
        tail = extra[:2, : c_rows * own_columns].reshape(2 * c_rows, own_columns)
        tail = jnp.concatenate((tail, jnp.zeros((EXTRA - 2 * c_rows, own_columns), BF16)))
        chunks = whole.reshape(sections, groups * rows, own_columns)
        chunks = [jnp.concatenate((part, tail)) for part in chunks]
        own_gain = lax.dynamic_slice_in_dim(
            enc_gain, (section * groups + mp) * own_columns, own_columns, 0
        ).reshape(1, 1, own_columns)

    attended, query_grad = mix(low, values), mix(grad_low, keys)
    first, *got = swap(2, chunks)
    first, attended, query_grad = lax.optimization_barrier((first, attended, query_grad))
    own_total, *parts, tail = sum_chunks([first] + got[::-1], groups, rows, c_rows)
    parts = swap(1, [own_total] + parts)[:0:-1]
    gain_own = gain_part(own_total, parts, hidden, inverse)
    if replicas == 2:
        gain_other = lax.ppermute(gain_own, "dp", [(0, 1), (1, 0)])
    else:
        gain_other = lax.psum(gain_own, "dp")
        gain_own = jnp.zeros_like(gain_own)
    hidden_grad = finish(own_total, tail, parts, hidden, own_gain, inverse, width, c_rows, direct, slots)
    gain_total = add_gain(gain_own, gain_other, replicas)
    return (
        attended[None, None],
        query_grad[None, None],
        hidden_grad[None],
        gain_total[0],
    )


def solution(mesh):
    in_specs = (
        P("dp", None, ("section", "mp")),
        P(),
        P("section", None, "mp"),
        P("section", None, "mp"),
        P("dp", "section", None, "mp"),
        P("dp", "section", None, "mp"),
    )
    out_specs = (
        P("dp", "section", None, "mp"),
        P("dp", "section", None, "mp"),
        P("dp", None, ("section", "mp")),
        P(("section", "mp")),
    )
    return jax.shard_map(
        per_device, mesh=mesh, in_specs=in_specs, out_specs=out_specs, check_vma=False
    )
```

```python
import math

import jax
import jax.numpy as jnp
from jax import lax
from jax.experimental import pallas as pl
from jax.experimental.pallas import tpu as pltpu
from jax.sharding import PartitionSpec as P

DH = 64
EPSILON = 1e-06
BLOCK = 256
EXTRA = 16
EXTRA_WIDTH = 256
PAD = 16
F32 = jnp.float32
BF16 = jnp.bfloat16
VMEM = pl.BlockSpec(memory_space=pltpu.VMEM)
SMEM = pl.BlockSpec(memory_space=pltpu.SMEM)
HBM = pl.BlockSpec(memory_space=pltpu.HBM)

NN = (((1,), (0,)), ((), ()))
NT = (((1,), (1,)), ((), ()))


def dot(a, b, dims=NN):
    return lax.dot_general(a, b, dims, preferred_element_type=F32)


def split_rows(row):
    high = row.astype(BF16)
    low = (row - high.astype(F32)).astype(BF16)
    return high, low


def in_vmem(array):
    return pltpu.with_memory_space_constraint(array, pltpu.VMEM)


def cost(flops, size):
    return pl.CostEstimate(flops=flops, bytes_accessed=size, transcendentals=0)


def in_hbm(array):
    return pltpu.with_memory_space_constraint(array, pltpu.HBM)


def block_at(direct, j, i, slots):
    if not direct:
        return j * slots + i
    section, mp, core = (lax.axis_index(name) for name in ("section", "mp", "dp"))
    turn = lax.rem(core, 2) * (i - j)
    return lax.bitwise_xor(section, j + turn) * slots + lax.bitwise_xor(mp, i - turn)


def fetch(arrays, weights, sections, slots, direct):
    width, columns = weights[0].shape
    block = width // (sections * slots)
    few, many = len(arrays), len(weights)

    def kernel(*refs):
        ins, outs, sems = refs[:few + many], refs[few + many:-1], refs[-1]
        copies = [pltpu.make_async_copy(ins[n], outs[n], sems.at[many, n]) for n in range(few)]
        for j in range(sections):
            for i in range(slots):
                row = pl.multiple_of(block_at(direct, j, i, slots) * block, block)
                n = j * slots + i
                copies += [
                    pltpu.make_async_copy(
                        ins[few + w].at[pl.ds(row, block), :], outs[few + w].at[n], sems.at[w, n]
                    )
                    for w in range(many)
                ]
        for copy in copies:
            copy.start()
        for copy in copies:
            copy.wait()

    return pl.pallas_call(
        kernel,
        out_shape=tuple(pltpu.VMEM(array.shape, array.dtype) for array in arrays)
        + (pltpu.VMEM((sections * slots, block, columns), BF16),) * many,
        in_specs=[HBM] * (few + many),
        out_specs=(VMEM,) * (few + many),
        scratch_shapes=[pltpu.SemaphoreType.DMA((many + 1, sections * slots))],
        compiler_params=pltpu.CompilerParams(vmem_limit_bytes=1 << 20),
        cost_estimate=cost(0, 4 * many * width * columns),
        name="fetch",
    )(*map(in_hbm, (*arrays, *weights)))


def attend(x, gain, wk, wv, q, g, direct):
    sections = len(x)
    flat = [array for arrays in x for array in arrays]
    _, rows, block = flat[0].shape
    slots = sum(array.shape[0] for array in x[0])
    length, columns = q.shape
    width = sections * slots * block
    pair = 2 * DH
    pairs = columns // pair
    factor = DH ** (-0.5)

    def kernel(*refs):
        x_refs, refs = refs[:len(flat)], refs[len(flat):]
        (gain_ref, wk_ref, wv_ref, q_ref, g_ref, low_ref, grad_low_ref, keys_ref, values_ref,
         kg_ref, vg_ref, inverse_ref, extra_ref, memory_buf) = refs
        places = [(ref, i) for ref in x_refs for i in range(ref.shape[0])]

        def wide(j, i):
            ref, n = places[j * slots + i]
            return ref[n].astype(F32)

        squares = jnp.zeros((rows, block), F32)
        for j in range(sections):
            for i in range(slots):
                squares += wide(j, i) * wide(j, i)
        inverse = lax.rsqrt(jnp.sum(squares, axis=-1, keepdims=True) / width + EPSILON)
        inverse_ref[...] = jnp.broadcast_to(inverse, inverse_ref.shape)

        keys = jnp.zeros((rows, columns), F32)
        values = jnp.zeros((rows, columns), F32)
        for j in range(sections):
            for i in range(slots):
                memory = wide(j, i) * inverse * gain_ref[block_at(direct, j, i, slots)]
                memory_buf[:, i * block:(i + 1) * block] = memory.astype(BF16)
            span = slice(j * slots, (j + 1) * slots)
            keys += dot(memory_buf[...], wk_ref[span].reshape(slots * block, columns))
            values += dot(memory_buf[...], wv_ref[span].reshape(slots * block, columns))
        keys_ref[...] = keys.astype(BF16)
        values_ref[...] = values.astype(BF16)

        first = lax.broadcasted_iota(jnp.int32, (rows, pair), 1) < DH
        zero = jnp.zeros((rows, pair), BF16)
        c_sum = jnp.zeros((rows, pair), F32)
        for p in range(pairs):
            at = slice(p * pair, (p + 1) * pair)
            k, v = keys_ref[:, at], values_ref[:, at]
            q, g = q_ref[:, at], g_ref[:, at]
            k_two = jnp.concatenate((jnp.where(first, k, zero), jnp.where(first, zero, k)), axis=0)
            v_two = jnp.concatenate((jnp.where(first, v, zero), jnp.where(first, zero, v)), axis=0)
            scores = dot(k_two, q, NT)
            share_grad = dot(v_two, g, NT)
            for h in range(2):
                head = slice(h * rows, (h + 1) * rows)
                score = scores[head]
                raised = jnp.exp((score - jnp.max(score, axis=0, keepdims=True)) * factor)
                shares = raised * (1.0 / jnp.sum(raised, axis=0, keepdims=True))
                low_ref[p, head, :] = shares.astype(BF16)
                grads = share_grad[head]
                mean = jnp.sum(shares * grads, axis=0, keepdims=True)
                grad_low_ref[p, head, :] = (shares * (grads - mean) * factor).astype(BF16)
            vg = dot(low_ref[p], g)
            kg = dot(grad_low_ref[p], q)
            vg = jnp.where(first, vg[:rows], vg[rows:]).astype(BF16)
            kg = jnp.where(first, kg[:rows], kg[rows:]).astype(BF16)
            vg_ref[:, at] = vg
            kg_ref[:, at] = kg
            c_sum += kg.astype(F32) * k.astype(F32) + vg.astype(F32) * v.astype(F32)

        row = jnp.sum(c_sum.T, axis=0, keepdims=True)
        row = jnp.concatenate((row, jnp.zeros((1, EXTRA_WIDTH - rows), F32)), axis=1)
        high, low = split_rows(row)
        blank = jnp.zeros((EXTRA - 2, EXTRA_WIDTH), BF16)
        extra_ref[...] = jnp.concatenate((high, low, blank), axis=0)

    return pl.pallas_call(
        kernel,
        out_shape=(
            pltpu.VMEM((pairs, 2 * rows, length), BF16),
            pltpu.VMEM((pairs, 2 * rows, length), BF16),
            pltpu.VMEM((rows, columns), BF16),
            pltpu.VMEM((rows, columns), BF16),
            pltpu.VMEM((rows, columns), BF16),
            pltpu.VMEM((rows, columns), BF16),
            pltpu.VMEM((rows, 128), F32),
            pltpu.VMEM((EXTRA, EXTRA_WIDTH), BF16),
        ),
        in_specs=[VMEM] * (len(flat) + 5),
        out_specs=(VMEM,) * 8,
        scratch_shapes=[pltpu.VMEM((rows, slots * block), BF16)],
        compiler_params=pltpu.CompilerParams(vmem_limit_bytes=16 << 20),
        cost_estimate=pl.CostEstimate(
            flops=4 * rows * width * columns + 16 * length * rows * columns,
            bytes_accessed=8 * width * columns,
            transcendentals=length * rows * columns // DH,
        ),
        name="attend",
    )(*flat, in_vmem(gain), in_vmem(wk), in_vmem(wv), q, g)


def mix(shares, weights):
    pairs, both, length = shares.shape
    rows, columns = weights.shape
    pair = columns // pairs

    def kernel(shares_ref, weights_ref, out_ref):
        first = lax.broadcasted_iota(jnp.int32, (rows, pair), 1) < DH
        zero = jnp.zeros((rows, pair), BF16)
        for p in range(pairs):
            at = slice(p * pair, (p + 1) * pair)
            w = weights_ref[:, at]
            two = jnp.concatenate((jnp.where(first, w, zero), jnp.where(first, zero, w)), axis=0)
            out_ref[:, at] = dot(two.T, shares_ref[p]).T.astype(BF16)

    return pl.pallas_call(
        kernel,
        out_shape=jax.ShapeDtypeStruct((length, columns), BF16),
        in_specs=[VMEM] * 2,
        out_specs=VMEM,
        compiler_params=pltpu.CompilerParams(vmem_limit_bytes=4 << 20),
        cost_estimate=cost(1, 1),
        name="mix",
    )(in_vmem(shares), in_vmem(weights))


def project(kg, vg, wk, wv, start, count, extra=None, size=0):
    rows, columns = kg.shape
    block = wk.shape[1]
    tail = [] if extra is None else [in_vmem(extra)]
    end = count * rows + EXTRA * len(tail)
    size = max(size, end)

    def kernel(kg_ref, vg_ref, wk_ref, wv_ref, *refs):
        kg, vg, out_ref = kg_ref[...], vg_ref[...], refs[-1]
        for i in range(count):
            part = dot(kg, wk_ref[start + i], NT) + dot(vg, wv_ref[start + i], NT)
            out_ref[i * rows:(i + 1) * rows, :] = part.astype(BF16)
        if tail:
            out_ref[count * rows:end, :] = refs[0][...]
        if size > end:
            out_ref[end:, :] = jnp.zeros((size - end, block), BF16)

    return pl.pallas_call(
        kernel,
        out_shape=pltpu.VMEM((size, block), BF16),
        in_specs=[VMEM] * (4 + len(tail)),
        out_specs=VMEM,
        compiler_params=pltpu.CompilerParams(vmem_limit_bytes=4 << 20),
        cost_estimate=cost(1, 1),
        name="project",
    )(in_vmem(kg), in_vmem(vg), in_vmem(wk), in_vmem(wv), *tail)


def join(parts, order):
    def kernel(*refs):
        for n, ref in zip(order, refs[:-1]):
            refs[-1][n] = ref[0]

    return pl.pallas_call(
        kernel,
        out_shape=pltpu.VMEM((len(parts), *parts[0].shape[1:]), BF16),
        in_specs=[VMEM] * len(parts),
        out_specs=VMEM,
        compiler_params=pltpu.CompilerParams(vmem_limit_bytes=2 << 20),
        name="join",
    )(in_vmem(parts[0]), *parts[1:])


def total_of(refs, start, size):
    total = refs[0][start:start + size, :].astype(F32)
    for ref in refs[1:]:
        total += ref[start:start + size, :].astype(F32)
    return total


def sum_c(extra, c_rows):
    return extra[:c_rows] + extra[c_rows:2 * c_rows]


def c_tail(c):
    high, low = split_rows(c)
    blank = jnp.zeros((EXTRA - 2 * c.shape[0], c.shape[1]), BF16)
    return jnp.concatenate((high, low, blank), axis=0)


def sum_chunks(chunks, count, rows, c_rows):
    block = chunks[0].shape[1]

    def kernel(*refs):
        parts, outs = refs[:len(chunks)], refs[len(chunks):]
        tail = c_tail(sum_c(total_of(parts, count * rows, EXTRA), c_rows))
        outs[-1][...] = tail
        outs[0][...] = total_of(parts, 0, rows)
        for i in range(1, count):
            outs[i][:rows, :] = total_of(parts, i * rows, rows).astype(BF16)
            outs[i][rows:, :] = tail

    return pl.pallas_call(
        kernel,
        out_shape=(pltpu.VMEM((rows, block), F32),)
        + (pltpu.VMEM((rows + EXTRA, block), BF16),) * (count - 1)
        + (pltpu.VMEM((EXTRA, block), BF16),),
        in_specs=[VMEM] * len(chunks),
        out_specs=(VMEM,) * (count + 1),
        compiler_params=pltpu.CompilerParams(vmem_limit_bytes=4 << 20),
        name="sum_chunks",
    )(*chunks)


def gain_part(own_total, parts, hidden, inverse):
    rows, block = own_total.shape

    def kernel(hidden_ref, inverse_ref, own_ref, *refs):
        part_refs, out_ref = refs[:-1], refs[-1]
        total = own_ref[...] + total_of(part_refs, 0, rows)
        normed = hidden_ref[0].astype(F32) * inverse_ref[:, 0:1]
        out_ref[...] = jnp.sum(total * normed, axis=0, keepdims=True)

    return pl.pallas_call(
        kernel,
        out_shape=pltpu.VMEM((1, block), F32),
        in_specs=[VMEM] * (3 + len(parts)),
        out_specs=VMEM,
        compiler_params=pltpu.CompilerParams(vmem_limit_bytes=4 << 20),
        name="gain_part",
    )(in_vmem(hidden), in_vmem(inverse), in_vmem(own_total), *parts)


def finish(own_total, tail, parts, hidden, gain, inverse, width, c_rows, direct, slots):
    rows, block = own_total.shape

    def kernel(hidden_ref, gain_ref, inverse_ref, own_ref, tail_ref, *refs):
        part_refs, out_ref = refs[:-1], refs[-1]
        extra = tail_ref[...].astype(F32) + total_of(part_refs, rows, EXTRA)
        c = sum_c(extra, c_rows)
        c = jnp.concatenate([c[n:n + 1] for n in range(c_rows)], axis=1)[:, :rows]
        mean = (jnp.broadcast_to(c, (rows, rows)) / width).T[:, 0:1]
        total = own_ref[...] + total_of(part_refs, 0, rows)
        inverse = inverse_ref[:, 0:1]
        normed = hidden_ref[0].astype(F32) * inverse
        out_ref[...] = inverse * (total * gain_ref[block_at(direct, 0, 0, slots)] - normed * mean)

    return pl.pallas_call(
        kernel,
        out_shape=jax.ShapeDtypeStruct((rows, block), F32),
        in_specs=[VMEM] * (5 + len(parts)),
        out_specs=VMEM,
        compiler_params=pltpu.CompilerParams(vmem_limit_bytes=4 << 20),
        cost_estimate=cost(0, 64 << 10),
        name="finish",
    )(in_vmem(hidden), in_vmem(gain), in_vmem(inverse), in_vmem(own_total), in_vmem(tail), *parts)


def add_gain(mine, theirs, replicas):
    def kernel(mine_ref, theirs_ref, out_ref):
        out_ref[...] = (mine_ref[...] + theirs_ref[...]) / replicas

    return pl.pallas_call(
        kernel,
        out_shape=jax.ShapeDtypeStruct(mine.shape, F32),
        in_specs=[VMEM, VMEM],
        out_specs=VMEM,
        compiler_params=pltpu.CompilerParams(vmem_limit_bytes=1 << 20),
        name="add_gain",
    )(in_vmem(mine), theirs)


def exchange(array, step, j, direct):
    names = ("section", "dp", "mp")
    sizes = [lax.axis_size(name) for name in names]
    pairs = []
    for n in range(math.prod(sizes)):
        section, core, mp = n // (sizes[1] * sizes[2]), n // sizes[2] % sizes[1], n % sizes[2]
        if (step == 2) != (direct and core % 2 == 1):
            section ^= j
        else:
            mp ^= j
        pairs.append((n, (section * sizes[1] + core) * sizes[2] + mp))
    return lax.ppermute(array, names, pairs)


def swapped(array, axis, mine):
    return jnp.stack(
        [
            lax.dynamic_index_in_dim(array, jnp.bitwise_xor(mine, i), axis, False)
            for i in range(array.shape[axis])
        ],
        axis,
    )


def per_device(enc_hidden, enc_gain, key_weight, value_weight, queries, out_grad):
    own = enc_hidden[0]
    rows, own_columns = own.shape
    wk, wv = key_weight[0], value_weight[0]
    width, columns = wk.shape
    sections = lax.axis_size("section")
    groups = lax.axis_size("mp")
    replicas = lax.axis_size("dp")
    section = lax.axis_index("section")
    mp = lax.axis_index("mp")
    direct = own_columns == BLOCK and sections == groups
    c_rows = max(rows // own_columns, 1)

    slots = groups if direct else 4

    def swap(step, arrays):
        got = [exchange(array, step, j, direct) for j, array in enumerate(arrays) if j]
        return [arrays[0]] + got

    gain = enc_gain.reshape(width // BLOCK, 1, BLOCK)
    parts = width // (slots * BLOCK)
    hidden, gain, wk = fetch((own[None], gain), (wk,), parts, slots, direct)
    (wv,) = fetch((), (wv,), parts, slots, direct)
    column = [hidden] + swap(1, [own[None]] * groups)[1:]
    order = sorted(range(groups), key=lambda j: (j > 0, j != 3, j))
    x = join([column[j] for j in order], order)
    if direct:
        x = [(part,) for part in swap(2, [x] * sections)]
    else:
        x = lax.all_gather(x, "section", axis=0)
        x = swapped(x, 1, mp).transpose(2, 0, 1, 3).reshape(rows, -1, slots, BLOCK)
        x = [(part,) for part in x.transpose(1, 2, 0, 3)]
    low, grad_low, keys, values, kg, vg, inverse, extra = attend(
        x, gain, wk, wv, queries[0, 0], out_grad[0, 0], direct
    )

    if direct:
        own_gain = gain
        size = {sections - 1: slots * rows + EXTRA + PAD}
        chunks = {
            j: project(kg, vg, wk, wv, j * slots, slots, extra, size.get(j, 0))
            for j in (0, *range(sections - 1, 0, -1))
        }
        chunks = [chunks[j] for j in range(sections)]
    else:
        whole = [
            project(kg, vg, wk, wv, n, 1) for n in range(width // BLOCK)
        ]
        whole = jnp.stack(whole).transpose(1, 0, 2)
        whole = whole.reshape(rows, sections, groups, own_columns).transpose(1, 2, 0, 3)
        whole = swapped(swapped(whole, 1, mp), 0, section)
        tail = extra[:2, : c_rows * own_columns].reshape(2 * c_rows, own_columns)
        tail = jnp.concatenate((tail, jnp.zeros((EXTRA - 2 * c_rows, own_columns), BF16)))
        chunks = whole.reshape(sections, groups * rows, own_columns)
        chunks = [jnp.concatenate((part, tail)) for part in chunks]
        own_gain = lax.dynamic_slice_in_dim(
            enc_gain, (section * groups + mp) * own_columns, own_columns, 0
        ).reshape(1, 1, own_columns)

    attended = mix(low, values)
    first, *got = swap(2, chunks)
    first, attended = lax.optimization_barrier((first, attended))
    own_total, *parts, tail = sum_chunks([first] + got[::-1], groups, rows, c_rows)
    own_total, grad_low = lax.optimization_barrier((own_total, grad_low))
    query_grad = mix(grad_low, keys)
    own_total, query_grad = lax.optimization_barrier((own_total, query_grad))
    parts = swap(1, [own_total] + parts)[:0:-1]
    gain_own = gain_part(own_total, parts, hidden, inverse)
    if replicas == 2:
        gain_other = lax.ppermute(gain_own, "dp", [(0, 1), (1, 0)])
    else:
        gain_other = lax.psum(gain_own, "dp")
        gain_own = jnp.zeros_like(gain_own)
    hidden_grad = finish(own_total, tail, parts, hidden, own_gain, inverse, width, c_rows, direct, slots)
    gain_total = add_gain(gain_own, gain_other, replicas)
    return (
        attended[None, None],
        query_grad[None, None],
        hidden_grad[None],
        gain_total[0],
    )


def solution(mesh):
    in_specs = (
        P("dp", None, ("section", "mp")),
        P(),
        P("section", None, "mp"),
        P("section", None, "mp"),
        P("dp", "section", None, "mp"),
        P("dp", "section", None, "mp"),
    )
    out_specs = (
        P("dp", "section", None, "mp"),
        P("dp", "section", None, "mp"),
        P("dp", None, ("section", "mp")),
        P(("section", "mp")),
    )
    return jax.shard_map(
        per_device, mesh=mesh, in_specs=in_specs, out_specs=out_specs, check_vma=False
    )
```
